512 devices in a mesh: tm: 128 (over x_hi, z, y), lat: 4 (over x_lo, core).
Axes of the slice: x: 4 (x_hi: 2, x_lo: 2; x = x_hi * 2 + x_lo), y: 8, z: 8, core: 2. Of those that a mesh axis runs over, the one named last changes fastest.
Arguments:
- increments: float32 [128, 4, 32, 384], P('tm', None, 'lat'), may hold values from -6 to 6
- correlation: float32 [128, 4, 32, 384], P('tm', None, 'lat'), may hold values from 0.3 to 1, as said below
- coefficients: float32 [6, 32, 384], P(None, 'lat'), may hold values from -0.15 to 0.2, as said below
- obs_cell: int32 [128, 4096], P('tm', 'lat'), may hold values from 0 to 49151
- obs_value: float32 [128, 4096], P('tm', 'lat'), may hold values from -6 to 6
- obs_weight: float32 [128, 4096], P('tm', 'lat'), may hold values from 0.5 to 4
- obs_count: int32 [128, 4], P('tm', 'lat'), may hold values from 512 to 1024, as said below
- obs_step: int32 [128], P('tm'), may hold values from 1 to 4
Outputs:
- gradient: float32 [128, 4, 32, 384], P('tm', None, 'lat')
- direction: float32 [128, 4, 32, 384], P('tm', None, 'lat')
The draws below stay inside these ranges and needn't reach their ends.
Inputs may be any that keep to these rules, and one draw needn't show every extreme that they name: `correlation`: per cell rates of several magnitudes, varying between subwindows. Positive wave coefficients and diffusivities, drifts of either sign. `obs_count`: in every subwindow some slab has all 1024 slots live.
All inputs are finite; a program needn't handle non-finite values.
Results may differ from the reference program's by a relative error of at most 0.0003.
Values sent between devices are 32-bit elements; how exact they have to be, the bound alone decides.
No kernel may reach another device: no remote copies, remote signals or barrier semaphores. Data moves between devices by JAX's collectives and lax.ppermute only.
A program may use at most 128 MiB of HBM per device.

```python
import math
import jax
import jax.numpy as jnp
from jax import lax

FIELDS = 4
LON = 384
STEPS = 4
NOBS = 1024
INTERVAL_NUMBER = 128
SLABS = 4
NY = 32
OBS_ALL = 4096


def draw_correlation(key, part):
    key = jax.random.fold_in(key, 11)
    steady_random_seeds, changing_random_seeds, spike_random_seeds = jax.random.split(key, 3)
    tensor_dimensions = (INTERVAL_NUMBER, FIELDS, NY, LON)
    low = math.log(0.3 / INTERVAL_NUMBER)
    high = math.log(0.1)
    steady_random_draw = jnp.exp(jax.random.uniform(steady_random_seeds, (1, FIELDS, NY, LON), jnp.float32, low, high))
    amplitude_multiplier = jnp.exp(jax.random.uniform(changing_random_seeds, tensor_dimensions, jnp.float32, math.log(0.5), math.log(2.0)))
    spike_random_draw = jax.random.uniform(spike_random_seeds, tensor_dimensions, jnp.float32) < 3.0 / INTERVAL_NUMBER
    return jnp.exp(-steady_random_draw * amplitude_multiplier) * jnp.where(spike_random_draw, 0.6, 1.0)


def draw_coefficients(key, part):
    key = jax.random.fold_in(key, 23)
    keys = jax.random.split(key, 6)
    tensor_dimensions = (NY, LON)
    drift = 0.1
    diff_low = 0.01
    wave_x = jnp.exp(jax.random.uniform(keys[0], tensor_dimensions, jnp.float32, math.log(0.02), math.log(0.2)))
    wave_y = jnp.exp(jax.random.uniform(keys[1], tensor_dimensions, jnp.float32, math.log(0.02), math.log(0.2)))
    drift_x = jax.random.uniform(keys[2], tensor_dimensions, jnp.float32, -drift, drift)
    drift_y = jax.random.uniform(keys[3], tensor_dimensions, jnp.float32, -drift, drift)
    diff_x = jnp.exp(jax.random.uniform(keys[4], tensor_dimensions, jnp.float32, math.log(diff_low), math.log(0.1)))
    diff_y = jnp.exp(jax.random.uniform(keys[5], tensor_dimensions, jnp.float32, math.log(diff_low), math.log(0.1)))
    return jnp.stack([wave_x, wave_y, drift_x, drift_y, diff_x, diff_y])


def draw_obs_count(key, part):
    key = jax.random.fold_in(key, 37)
    key_count, key_full = jax.random.split(key)
    counts = jax.random.randint(key_count, (INTERVAL_NUMBER, SLABS), NOBS // 2, NOBS + 1)
    full_slab = jax.random.randint(key_full, (INTERVAL_NUMBER, 1), 0, SLABS)
    slab_ids = jnp.arange(SLABS, dtype=jnp.int32)[None, :]
    return jnp.where(slab_ids == full_slab, NOBS, counts).astype(jnp.int32)


def set_ends(values, rng, smallest, top_value):
    extent = values.shape
    place = [jax.random.randint(jax.random.fold_in(rng, axis), (), 0, extent[axis]) for axis in range(len(extent))]
    values = values.at[tuple(place)].set(smallest)
    longest = extent.index(max(extent))
    place[longest] = (place[longest] + 1) % extent[longest]
    return values.at[tuple(place)].set(top_value)


def levels(own_key, shape, cuts, low, top_value):
    def one(dim, shards_of):
        steps = jax.random.uniform(jax.random.fold_in(jax.random.fold_in(own_key, 6), dim), (shards_of,), jnp.float32, low / len(cuts), top_value / len(cuts))
        return jnp.repeat(jnp.exp(steps), shape[dim] // shards_of).reshape((-1,) + (1,) * (len(shape) - dim - 1))

    gain = one(*cuts[0])
    for cut in cuts[1:]:
        gain = gain * one(*cut)
    return gain


def gaussian(stream_key, shape, width, limit, shards=(), kind=jnp.bfloat16):
    values = jax.random.normal(stream_key, shape, jnp.float32) * width
    if len(shards) > 0:
        values = levels(stream_key, shape, shards, -0.22, 0.18) * values
    return jnp.clip(values, min=-limit, max=limit).astype(kind)


def setup_inputs(seed: int = 0) -> dict:
    streams_of = jax.random.split(jax.random.key(seed), 9)
    increments = gaussian(streams_of[0], (INTERVAL_NUMBER, FIELDS, NY, LON), 1.0, 6.0, ((0, 128), (2, 4)), jnp.float32)
    correlation = draw_correlation(jax.random.fold_in(streams_of[8], 71), 0)
    coefficients = draw_coefficients(jax.random.fold_in(streams_of[8], 71), 0)
    obs_cell = set_ends(jax.random.randint(streams_of[3], (INTERVAL_NUMBER, OBS_ALL), 0, FIELDS * NY * LON), jax.random.fold_in(streams_of[3], 1), 0, (FIELDS * NY * LON) - 1).astype(jnp.int32)
    obs_value = gaussian(streams_of[4], (INTERVAL_NUMBER, OBS_ALL), 1.0, 6.0, ((0, 128), (1, 4)), jnp.float32)
    obs_weight = jnp.clip(jnp.exp(math.log(4.0) - 2.0794415 * jax.random.uniform(streams_of[5], (INTERVAL_NUMBER, OBS_ALL), jnp.float32) ** levels(streams_of[5], (INTERVAL_NUMBER, OBS_ALL), ((0, 128), (1, 4)), -0.2, 0.2)), 0.5, 4.0)
    obs_count = draw_obs_count(jax.random.fold_in(streams_of[8], 71), 0)
    obs_step = set_ends(jax.random.randint(streams_of[7], (INTERVAL_NUMBER,), 1, STEPS + 1), jax.random.fold_in(streams_of[7], 1), 1, STEPS).astype(jnp.int32)
    return dict(increments=increments, correlation=correlation, coefficients=coefficients, obs_cell=obs_cell, obs_value=obs_value, obs_weight=obs_weight, obs_count=obs_count, obs_step=obs_step)


def eastward(field):
    return jnp.roll(field, -1, axis=-1)


def westward(field):
    return jnp.roll(field, 1, axis=-1)


def diffuse(field, diff_x, diff_y):
    flux_x = diff_x * (eastward(field) - field)
    along_x = flux_x - westward(flux_x)
    flux_y = diff_y[:-1] * (field[1:] - field[:-1])
    return along_x[1:-1] + flux_y[1:] - flux_y[:-1]


def stencil(padded, coef_pad, sign):
    height = padded[0]
    zonal = padded[1]
    meridional = padded[2]
    tracer = padded[3]
    wave_x = coef_pad[0]
    wave_y = coef_pad[1]
    drift_x = coef_pad[2]
    drift_y = coef_pad[3]
    diff_x = coef_pad[4]
    diff_y = coef_pad[5]
    flow_x = wave_x * zonal
    flow_y = wave_y * meridional
    divergence = (westward(flow_x) - flow_x)[1:-1] + flow_y[:-2] - flow_y[1:-1]
    slope_x = (wave_x * (eastward(height) - height))[1:-1]
    slope_y = wave_y[1:-1] * (height[2:] - height[1:-1])
    carried_x = drift_x * tracer
    carried_y = drift_y * tracer
    transport = (drift_x * eastward(tracer) - westward(carried_x))[1:-1] + drift_y[1:-1] * tracer[2:] - carried_y[:-2]
    new_height = height[1:-1] + sign * divergence + diffuse(height, diff_x, diff_y)
    new_zonal = zonal[1:-1] - sign * slope_x + diffuse(zonal, diff_x, diff_y)
    new_meridional = meridional[1:-1] - sign * slope_y + diffuse(meridional, diff_x, diff_y)
    new_tracer = tracer[1:-1] - sign * transport + diffuse(tracer, diff_x, diff_y)
    return jnp.stack([new_height, new_zonal, new_meridional, new_tracer])


def pad_rows(field):
    return jnp.pad(field, ((0, 0), (1, 1), (0, 0)))


def reference(increments, correlation, coefficients, obs_cell, obs_value, obs_weight, obs_count, obs_step):
    coef_pad = pad_rows(coefficients)

    def forward(inputs):
        state, obs_at = inputs
        seen = jnp.zeros_like(state)
        for turn in range(STEPS):
            state = stencil(pad_rows(state), coef_pad, 1.0)
            seen = jnp.where(obs_at == turn + 1, state, seen)
        return state, seen

    ends, seen = lax.map(forward, (increments, obs_step))
    slots = jnp.arange(NOBS, dtype=jnp.int32)
    valid = (slots[None, None, :] < obs_count[:, :, None]).reshape(INTERVAL_NUMBER, OBS_ALL)
    sampled = jnp.take_along_axis(seen.reshape(INTERVAL_NUMBER, -1), obs_cell, axis=1)
    depart = jnp.where(valid, obs_weight * (sampled - obs_value), 0.0)
    zero_state = jnp.zeros_like(increments[:1])
    misfit = increments - jnp.concatenate([zero_state, ends[:-1]], axis=0)
    following = jnp.concatenate([misfit[1:], zero_state], axis=0)

    def backward(inputs):
        ahead, cells, weighted, obs_at = inputs
        inject = jnp.zeros((FIELDS * NY * LON,), jnp.float32).at[cells].add(weighted).reshape(FIELDS, NY, LON)
        adjoint = -ahead + jnp.where(obs_at == STEPS, inject, 0.0)
        for turn in range(STEPS):
            adjoint = stencil(pad_rows(adjoint), coef_pad, -1.0)
            adjoint = adjoint + jnp.where(obs_at == STEPS - 1 - turn, inject, 0.0)
        return adjoint

    adjoint = lax.map(backward, (following, obs_cell, depart, obs_step))
    gradient = misfit + adjoint

    def back_step(carry, inputs):
        term, rates = inputs
        summed = term + carry
        return rates * summed, summed

    _, summed = lax.scan(back_step, jnp.zeros_like(increments[0]), (gradient, correlation), reverse=True)

    def ahead_step(carry, inputs):
        term, rates = inputs
        smooth = rates * carry + (1.0 - rates * rates) * term
        return smooth, smooth

    _, direction = lax.scan(ahead_step, jnp.zeros_like(increments[0]), (summed, correlation))
    return gradient, direction
```

```python
import jax
import jax.numpy as jnp
from jax import lax
from jax.experimental import pallas as pl
from jax.experimental.pallas import tpu as pltpu
from jax.sharding import PartitionSpec as P

STEPS = 4
FIELDS = 4
NY = 32
LON = 384
ROWS = 8
SLABS = 4
WIN = 3 * ROWS
MID = 16
LANE = 128
TILES = LON // LANE
PACK = 11 * ROWS
KINDS = 4
TIMES = 128
CHUNK = 256


def lon_roll(field, by):
    return pltpu.roll(field, by % LON, 1)


def row_roll(field, by):
    return pltpu.roll(field, by % WIN, 0)


def step(state, coef, sign):
    h, u, v, q = state
    keep, kx, kw, ky, ks, cx, cw, cy, cs = coef["common"]
    qe, qw, qn, qs = coef["forward" if sign > 0 else "backward"]

    def sides(f):
        return lon_roll(f, -1), lon_roll(f, 1), row_roll(f, -1), row_roll(f, 1)

    def spread(f, e, w, n, s):
        return keep * f + (kx * e + kw * w) + (ky * n + ks * s)

    he, hw, hn, hs = sides(h)
    ue, uw, un, us = sides(u)
    ve, vw, vn, vs = sides(v)
    te, tw, tn, ts = sides(q)
    div = (cw * uw - cx * u) + (cs * vs - cy * v)
    gx = cx * (he - h)
    gy = cy * (hn - h)
    new_h = spread(h, he, hw, hn, hs)
    new_u = spread(u, ue, uw, un, us)
    new_v = spread(v, ve, vw, vn, vs)
    new_q = keep * q + (qe * te + qw * tw) + (qn * tn + qs * ts)
    if sign > 0:
        return new_h + div, new_u - gx, new_v - gy, new_q
    return new_h - div, new_u + gx, new_v + gy, new_q


def split(value):
    big = value.astype(jnp.bfloat16)
    return big, (value - big.astype(jnp.float32)).astype(jnp.bfloat16)


def subwindow_kernel(obs_step, packed, rates, out, buf):
    slab = lax.axis_index("lat")
    obs_at = obs_step[0]

    def window(base):
        parts = []
        for offset in (-1, 0, 1):
            at = slab + offset
            inside = jnp.logical_and(at >= 0, at < SLABS)
            first = jnp.clip(at, 0, SLABS - 1) * PACK + base
            part = packed[pl.ds(pl.multiple_of(first, ROWS), ROWS), :]
            parts.append(jnp.where(inside, part, 0.0))
        return jnp.concatenate(parts, axis=0)

    row = lax.broadcasted_iota(jnp.int32, (WIN, LON), 0) + (slab - 1) * ROWS
    in_grid = jnp.logical_and(row >= 0, row < NY)
    inc = tuple(window(f * ROWS) for f in range(FIELDS))
    cx, cy, ax, by, kx, ky = (window((FIELDS + i) * ROWS) for i in range(6))

    def south(c):
        return jnp.where(in_grid, row_roll(c, 1), 0.0)

    kw, ks, cw, cs = lon_roll(kx, 1), south(ky), lon_roll(cx, 1), south(cy)
    aw, bs = lon_roll(ax, 1), south(by)
    keep = 1.0 - ((kx + kw) + (ky + ks))
    coef = {
        "common": (keep, kx, kw, ky, ks, cx, cw, cy, cs),
        "forward": (kx - ax, kw + aw, ky - by, ks + bs),
        "backward": (kx + ax, kw - aw, ky + by, ks - bs),
    }
    state = inc
    seen = inc
    for turn in range(STEPS):
        state = step(state, coef, 1.0)
        if turn == 0:
            seen = state
        else:
            seen = tuple(jnp.where(obs_at == turn + 1, a, b) for a, b in zip(state, seen, strict=True))
    end = state

    for f in range(FIELDS):
        buf[f * WIN : (f + 1) * WIN, :] = seen[f]
    edge = (WIN - MID) // 2
    table = jnp.concatenate(
        [
            buf[f * WIN + edge : f * WIN + edge + MID, t * LANE : (t + 1) * LANE]
            for t in range(TILES)
            for f in range(FIELDS)
        ],
        axis=0,
    )
    high = table.shape[0]
    table_parts = jnp.concatenate(split(table), axis=1)

    hi_iota = lax.broadcasted_iota(jnp.int32, (high, LANE), 0)
    lo_iota = lax.broadcasted_iota(jnp.int32, (LANE, LANE), 0)
    forcing = jnp.zeros((high, 2 * LANE), jnp.float32)
    for owner in range(SLABS):
        base = owner * PACK + 10 * ROWS
        cell = packed[base : base + ROWS, 0:LANE].astype(jnp.int32)
        value = packed[base : base + ROWS, LANE : 2 * LANE]
        weight = packed[base : base + ROWS, 2 * LANE : 3 * LANE]
        low = jnp.bitwise_and(cell, LANE - 1)
        tile_row = jnp.right_shift(cell, 7)
        field_row = jnp.right_shift(tile_row * 21846, 16)
        tile = tile_row - field_row * TILES
        field = jnp.right_shift(field_row, 5)
        rel = jnp.bitwise_and(field_row, NY - 1) - (slab * ROWS - edge)
        near = jnp.logical_and(rel >= 0, rel < MID)
        spot = jnp.where(near, tile * (FIELDS * MID) + field * MID + rel, -1)
        for pair in range(ROWS // 2):
            rows = (2 * pair, 2 * pair + 1)
            pick = jnp.concatenate(
                [jnp.where(hi_iota == spot[r : r + 1, :], 1.0, 0.0) for r in rows], axis=1
            ).astype(jnp.bfloat16)
            match = jnp.concatenate([lo_iota == low[r : r + 1, :] for r in rows], axis=1)
            columns = lax.dot_general(
                table_parts, pick, (((0,), (0,)), ((), ())), preferred_element_type=jnp.float32
            )
            columns = columns[:LANE] + columns[LANE:]
            sampled = jnp.sum(jnp.where(match, columns, 0.0), axis=0, keepdims=True)
            wide_value = jnp.concatenate([value[r : r + 1, :] for r in rows], axis=1)
            wide_weight = jnp.concatenate([weight[r : r + 1, :] for r in rows], axis=1)
            depart = wide_weight * (sampled - wide_value)
            rounded = depart.astype(jnp.bfloat16).astype(jnp.float32)
            placed = jnp.concatenate(
                [
                    jnp.where(match, rounded, 0.0).astype(jnp.bfloat16),
                    jnp.where(match, depart - rounded, 0.0).astype(jnp.bfloat16),
                ],
                axis=0,
            )
            forcing = forcing + lax.dot_general(
                pick, placed, (((1,), (1,)), ((), ())), preferred_element_type=jnp.float32
            )
    forcing = forcing[:, :LANE] + forcing[:, LANE:]

    back = inc
    for _ in range(STEPS):
        back = step(back, coef, -1.0)

    buf[...] = jnp.zeros_like(buf)
    for t in range(TILES):
        for f in range(FIELDS):
            first = (t * FIELDS + f) * MID
            buf[f * WIN + edge : f * WIN + edge + MID, t * LANE : (t + 1) * LANE] = forcing[
                first : first + MID, :
            ]
    inject = tuple(buf[f * WIN : (f + 1) * WIN, :] for f in range(FIELDS))

    def push(state, turn):
        scale = jnp.where(obs_at == turn, 1.0, 0.0)
        return tuple(a + scale * b for a, b in zip(state, inject, strict=True))

    follows = jnp.where(lax.axis_index("tm") < TIMES - 1, 1.0, 0.0)
    adjoint = push(tuple(follows * e for e in end), STEPS)
    for turn in range(STEPS):
        adjoint = push(step(adjoint, coef, -1.0), STEPS - 1 - turn)

    for f in range(FIELDS):
        mine = slice(ROWS, 2 * ROWS)
        kinds = (inc[f][mine] + adjoint[f][mine], -end[f][mine], -back[f][mine], rates[f])
        for q, kind in enumerate(kinds):
            for t in range(TILES):
                first = (t * FIELDS * ROWS + f * ROWS) * KINDS + q
                out[pl.ds(first, ROWS, stride=KINDS), :] = kind[:, t * LANE : (t + 1) * LANE]
    used = TILES * FIELDS * ROWS * KINDS
    out[used:, :] = jnp.zeros((TIMES * KINDS - used, LANE), jnp.float32)


def time_kernel(parts, out):
    spans, length = 8, TIMES // 8
    sub = lax.broadcasted_iota(jnp.int32, (spans, LANE), 0)

    def load(q):
        return [parts[pl.ds(i * KINDS + q, spans, stride=length * KINDS), :] for i in range(length)]

    def up(x, by, fill):
        return jnp.where(sub < spans - by, pltpu.roll(x, spans - by, 0), fill)

    def down(x, by, fill):
        return jnp.where(sub >= by, pltpu.roll(x, by, 0), fill)

    x, y, z, c = (load(q) for q in range(KINDS))
    y = [down(y[-1], 1, 0.0)] + y[:-1]
    z = z[1:] + [up(z[0], 1, 0.0)]
    g = [(a + b) + d for a, b, d in zip(x, y, z, strict=True)]

    part, factor = [None] * length, [None] * length
    part[-1], factor[-1] = g[-1], jnp.ones_like(g[-1])
    for i in range(length - 2, -1, -1):
        part[i] = g[i] + c[i + 1] * part[i + 1]
        factor[i] = c[i + 1] * factor[i + 1]
    a, b = c[0] * factor[0], c[0] * part[0]
    for by in (1, 2, 4):
        a, b = a * up(a, by, 1.0), b + a * up(b, by, 0.0)
    enter = up(b, 1, 0.0)
    total = [p + f * enter for p, f in zip(part, factor, strict=True)]

    term = [(1.0 - r * r) * s for r, s in zip(c, total, strict=True)]
    part, factor = [term[0]], [c[0]]
    for i in range(1, length):
        part.append(c[i] * part[-1] + term[i])
        factor.append(c[i] * factor[-1])
    a, b = factor[-1], part[-1]
    for by in (1, 2, 4):
        a, b = a * down(a, by, 1.0), b + a * down(b, by, 0.0)
    enter = down(b, 1, 0.0)
    for i in range(length):
        out[pl.ds(i * 2, spans, stride=length * 2), :] = g[i]
        out[pl.ds(i * 2 + 1, spans, stride=length * 2), :] = part[i] + factor[i] * enter


def unpack_kernel(parts, gradient, direction):
    for e, out in enumerate((gradient, direction)):
        for f in range(FIELDS):
            for t in range(TILES):
                first = (t * FIELDS * ROWS + f * ROWS) * 2 + e
                out[f, :, t * LANE : (t + 1) * LANE] = parts[pl.ds(first, ROWS, stride=2), :]


def on_device(
    increments, correlation, coefficients, obs_cell, obs_value, obs_weight, obs_count, obs_step
):
    slots = jnp.arange(obs_cell.shape[1], dtype=jnp.int32)
    weight = jnp.where(slots < obs_count[0, 0], obs_weight[0], 0.0)
    lists = [obs_cell[0].astype(jnp.float32), obs_value[0], weight]
    obs = jnp.concatenate([part.reshape(ROWS, LANE) for part in lists], axis=1)
    mine = jnp.concatenate(
        [increments.reshape(FIELDS * ROWS, LON), coefficients.reshape(6 * ROWS, LON), obs], axis=0
    )
    packed = lax.all_gather(mine, "lat", axis=0, tiled=True)

    vmem = pl.BlockSpec(memory_space=pltpu.VMEM)
    smem = pl.BlockSpec(memory_space=pltpu.SMEM)
    limit = pltpu.CompilerParams(vmem_limit_bytes=32 * 1024 * 1024)
    sent = pl.pallas_call(
        subwindow_kernel,
        out_shape=jax.ShapeDtypeStruct((TIMES * KINDS, LANE), jnp.float32),
        in_specs=[smem, vmem, vmem],
        out_specs=vmem,
        scratch_shapes=[pltpu.VMEM((FIELDS * WIN, LON), jnp.float32)],
        compiler_params=limit,
    )(obs_step, packed, correlation[0])
    owned = lax.all_to_all(sent, "tm", 0, 0, tiled=True)
    solved = pl.pallas_call(
        time_kernel,
        out_shape=jax.ShapeDtypeStruct((TIMES * 2, LANE), jnp.float32),
        in_specs=[vmem],
        out_specs=vmem,
        compiler_params=limit,
    )(owned)
    returned = lax.all_to_all(solved, "tm", 0, 0, tiled=True)
    shape = jax.ShapeDtypeStruct((FIELDS, ROWS, LON), jnp.float32)
    gradient, direction = pl.pallas_call(
        unpack_kernel,
        out_shape=(shape, shape),
        in_specs=[vmem],
        out_specs=(vmem, vmem),
        compiler_params=limit,
    )(returned)
    return gradient[None], direction[None]


def solution(mesh):
    return jax.shard_map(
        on_device,
        mesh=mesh,
        in_specs=(
            P("tm", None, "lat", None),
            P("tm", None, "lat", None),
            P(None, "lat", None),
            P("tm", "lat"),
            P("tm", "lat"),
            P("tm", "lat"),
            P("tm", "lat"),
            P("tm"),
        ),
        out_specs=(P("tm", None, "lat", None), P("tm", None, "lat", None)),
        check_vma=False,
    )
```

```python
import jax
import jax.numpy as jnp
from jax import lax
from jax.experimental import pallas as pl
from jax.experimental.pallas import tpu as pltpu
from jax.sharding import PartitionSpec as P

STEPS = 4
FIELDS = 4
NY = 32
LON = 384
ROWS = 8
SLABS = 4
WIN = 3 * ROWS
MID = 16
LANE = 128
TILES = LON // LANE
PACK = 11 * ROWS
KINDS = 4
TIMES = 128
SPAN = 16
BLOCKS = TIMES // SPAN
SHARE = FIELDS * ROWS * TILES // SPAN
MAPS = 8
CHUNK = 256


def lon_roll(field, by):
    return pltpu.roll(field, by % LON, 1)


def row_roll(field, by):
    return pltpu.roll(field, by % WIN, 0)


def step(state, coef, sign):
    h, u, v, q = state
    keep, kx, kw, ky, ks, cx, cw, cy, cs = coef["common"]
    qe, qw, qn, qs = coef["forward" if sign > 0 else "backward"]

    def sides(f):
        return lon_roll(f, -1), lon_roll(f, 1), row_roll(f, -1), row_roll(f, 1)

    def spread(f, e, w, n, s):
        return keep * f + (kx * e + kw * w) + (ky * n + ks * s)

    he, hw, hn, hs = sides(h)
    ue, uw, un, us = sides(u)
    ve, vw, vn, vs = sides(v)
    te, tw, tn, ts = sides(q)
    div = (cw * uw - cx * u) + (cs * vs - cy * v)
    gx = cx * (he - h)
    gy = cy * (hn - h)
    new_h = spread(h, he, hw, hn, hs)
    new_u = spread(u, ue, uw, un, us)
    new_v = spread(v, ve, vw, vn, vs)
    new_q = keep * q + (qe * te + qw * tw) + (qn * tn + qs * ts)
    if sign > 0:
        return new_h + div, new_u - gx, new_v - gy, new_q
    return new_h - div, new_u + gx, new_v + gy, new_q


def split(value):
    big = value.astype(jnp.bfloat16)
    return big, (value - big.astype(jnp.float32)).astype(jnp.bfloat16)


def pack_kernel(inc, coef, cell, value, weight, count, out, cell_buf, weight_buf, sems):
    first = (FIELDS + 6) * ROWS
    moves = (
        (cell, cell_buf),
        (weight, weight_buf),
        (coef, out.at[FIELDS * ROWS : first, :]),
        (inc, out.at[0 : FIELDS * ROWS, :]),
        (value, out.at[first:PACK, LANE : 2 * LANE]),
    )
    copies = [pltpu.make_async_copy(a, b, sems.at[i]) for i, (a, b) in enumerate(moves)]
    for copy in copies:
        copy.start()
    slot = lax.broadcasted_iota(jnp.int32, (ROWS, LANE), 0) * LANE
    slot = slot + lax.broadcasted_iota(jnp.int32, (ROWS, LANE), 1)
    live = slot < count[0, 0]
    for copy in copies[:2]:
        copy.wait()
    out[first:PACK, 0:LANE] = cell_buf[...].astype(jnp.float32)
    out[first:PACK, 2 * LANE :] = jnp.where(live, weight_buf[...], 0.0)
    for copy in copies[2:]:
        copy.wait()


def subwindow_kernel(obs_step, packed, rates, out, buf):
    slab = lax.axis_index("lat")
    obs_at = jnp.broadcast_to(obs_step[...], (WIN, LON))

    def window(base):
        parts = []
        for offset in (-1, 0, 1):
            at = slab + offset
            inside = jnp.logical_and(at >= 0, at < SLABS)
            first = jnp.clip(at, 0, SLABS - 1) * PACK + base
            part = packed[pl.ds(pl.multiple_of(first, ROWS), ROWS), :]
            parts.append(jnp.where(inside, part, 0.0))
        return jnp.concatenate(parts, axis=0)

    row = lax.broadcasted_iota(jnp.int32, (WIN, LON), 0) + (slab - 1) * ROWS
    in_grid = jnp.logical_and(row >= 0, row < NY)
    inc = tuple(window(f * ROWS) for f in range(FIELDS))
    cx, cy, ax, by, kx, ky = (window((FIELDS + i) * ROWS) for i in range(6))

    def south(c):
        return jnp.where(in_grid, row_roll(c, 1), 0.0)

    kw, ks, cw, cs = lon_roll(kx, 1), south(ky), lon_roll(cx, 1), south(cy)
    aw, bs = lon_roll(ax, 1), south(by)
    keep = 1.0 - ((kx + kw) + (ky + ks))
    coef = {
        "common": (keep, kx, kw, ky, ks, cx, cw, cy, cs),
        "forward": (kx - ax, kw + aw, ky - by, ks + bs),
        "backward": (kx + ax, kw - aw, ky + by, ks - bs),
    }
    state = inc
    seen = inc
    for turn in range(STEPS):
        state = step(state, coef, 1.0)
        if turn == 0:
            seen = state
        else:
            seen = tuple(jnp.where(obs_at == turn + 1, a, b) for a, b in zip(state, seen, strict=True))
    end = state

    for f in range(FIELDS):
        buf[f * WIN : (f + 1) * WIN, :] = seen[f]
    edge = (WIN - MID) // 2
    table = jnp.concatenate(
        [
            buf[f * WIN + edge : f * WIN + edge + MID, t * LANE : (t + 1) * LANE]
            for t in range(TILES)
            for f in range(FIELDS)
        ],
        axis=0,
    )
    high = table.shape[0]
    table_parts = jnp.concatenate(split(table), axis=1)

    hi_iota = lax.broadcasted_iota(jnp.int32, (high, LANE), 0)
    lo_iota = lax.broadcasted_iota(jnp.int32, (LANE, LANE), 0)
    forcing = jnp.zeros((high, 2 * LANE), jnp.float32)
    for owner in range(SLABS):
        base = owner * PACK + 10 * ROWS
        cell = packed[base : base + ROWS, 0:LANE].astype(jnp.int32)
        value = packed[base : base + ROWS, LANE : 2 * LANE]
        weight = packed[base : base + ROWS, 2 * LANE : 3 * LANE]
        low = jnp.bitwise_and(cell, LANE - 1)
        tile_row = jnp.right_shift(cell, 7)
        field_row = jnp.right_shift(tile_row * 21846, 16)
        tile = tile_row - field_row * TILES
        field = jnp.right_shift(field_row, 5)
        rel = jnp.bitwise_and(field_row, NY - 1) - (slab * ROWS - edge)
        near = jnp.logical_and(rel >= 0, rel < MID)
        spot = jnp.where(near, tile * (FIELDS * MID) + field * MID + rel, -1)
        for pair in range(ROWS // 2):
            rows = (2 * pair, 2 * pair + 1)
            pick = jnp.concatenate(
                [jnp.where(hi_iota == spot[r : r + 1, :], 1.0, 0.0) for r in rows], axis=1
            ).astype(jnp.bfloat16)
            match = jnp.concatenate([lo_iota == low[r : r + 1, :] for r in rows], axis=1)
            columns = lax.dot_general(
                table_parts, pick, (((0,), (0,)), ((), ())), preferred_element_type=jnp.float32
            )
            columns = columns[:LANE] + columns[LANE:]
            sampled = jnp.sum(jnp.where(match, columns, 0.0), axis=0, keepdims=True)
            wide_value = jnp.concatenate([value[r : r + 1, :] for r in rows], axis=1)
            wide_weight = jnp.concatenate([weight[r : r + 1, :] for r in rows], axis=1)
            depart = wide_weight * (sampled - wide_value)
            rounded = depart.astype(jnp.bfloat16).astype(jnp.float32)
            placed = jnp.concatenate(
                [
                    jnp.where(match, rounded, 0.0).astype(jnp.bfloat16),
                    jnp.where(match, depart - rounded, 0.0).astype(jnp.bfloat16),
                ],
                axis=0,
            )
            forcing = forcing + lax.dot_general(
                pick, placed, (((1,), (1,)), ((), ())), preferred_element_type=jnp.float32
            )
    forcing = forcing[:, :LANE] + forcing[:, LANE:]

    back = inc
    for _ in range(STEPS):
        back = step(back, coef, -1.0)

    buf[...] = jnp.zeros_like(buf)
    for t in range(TILES):
        for f in range(FIELDS):
            first = (t * FIELDS + f) * MID
            buf[f * WIN + edge : f * WIN + edge + MID, t * LANE : (t + 1) * LANE] = forcing[
                first : first + MID, :
            ]
    inject = tuple(buf[f * WIN : (f + 1) * WIN, :] for f in range(FIELDS))

    def push(state, turn):
        scale = jnp.where(obs_at == turn, 1.0, 0.0)
        return tuple(a + scale * b for a, b in zip(state, inject, strict=True))

    follows = jnp.where(lax.axis_index("tm") < TIMES - 1, 1.0, 0.0)
    adjoint = push(tuple(follows * e for e in end), STEPS)
    for turn in range(STEPS):
        adjoint = push(step(adjoint, coef, -1.0), STEPS - 1 - turn)

    mine = slice(ROWS, 2 * ROWS)
    for f in range(FIELDS):
        kinds = (inc[f][mine] + adjoint[f][mine], -end[f][mine], -back[f][mine], rates[f])
        half, odd = divmod(f, 2)
        for q, kind in enumerate(kinds):
            for t in range(TILES):
                first = half * ROWS * KINDS * SHARE + q * SHARE + odd * TILES + t
                out[pl.ds(first, ROWS, stride=KINDS * SHARE), :] = kind[:, t * LANE : (t + 1) * LANE]


def load_block(parts):
    def load(i, q):
        first = (i * KINDS + q) * SHARE
        return parts[first : first + SHARE, :]

    x, y, z, c = ([load(i, q) for i in range(SPAN)] for q in range(KINDS))
    g = list(x)
    for i in range(1, SPAN):
        g[i] = g[i] + y[i - 1]
        g[i - 1] = g[i - 1] + z[i]
    return g, y, z, c


def block_kernel(parts, out):
    g, y, z, c = load_block(parts)
    sums, factors = [g[-1]], [jnp.ones_like(g[-1])]
    for i in range(SPAN - 2, -1, -1):
        sums.insert(0, g[i] + c[i + 1] * sums[0])
        factors.insert(0, c[i + 1] * factors[0])
    shares = [1.0 - r * r for r in c]
    own, push = shares[0] * sums[0], shares[0] * factors[0]
    for i in range(1, SPAN):
        own = c[i] * own + shares[i] * sums[i]
        push = c[i] * push + shares[i] * factors[i]
    terms = (
        c[0] * factors[0],
        c[0],
        push,
        shares[0] * factors[0],
        c[0] * sums[0] + z[0],
        own,
        y[-1],
        z[0],
    )
    size = MAPS * SHARE
    for i, term in enumerate(terms):
        out[i * SHARE : (i + 1) * SHARE, :] = term
    whole = out[0:size, :]
    for b in range(1, BLOCKS):
        out[b * size : (b + 1) * size, :] = whole


def time_kernel(parts, maps, out):
    block = jnp.right_shift(lax.axis_index("tm"), 4)

    def term(b, i):
        first = (b * MAPS + i) * SHARE
        return maps[first : first + SHARE, :]

    through, first_rate, push, edge, back, own, last_y, first_z = (
        [term(b, i) for b in range(BLOCKS)] for i in range(MAPS)
    )
    zero = jnp.zeros_like(own[0])
    before = [zero] + last_y[:-1]
    after = first_z[1:] + [zero]
    later = [zero]
    for b in range(BLOCKS - 1, 0, -1):
        later.insert(0, (back[b] + first_rate[b] * before[b]) + through[b] * later[0])
    earlier = [zero]
    for b in range(BLOCKS - 1):
        made = (own[b] + push[b] * later[b]) + edge[b] * before[b]
        earlier.append(made + through[b] * earlier[-1])

    def mine(values):
        picked = values[0]
        for b in range(1, BLOCKS):
            picked = jnp.where(block == b, values[b], picked)
        return picked

    g, _, _, c = load_block(parts)
    g[0] = g[0] + mine(before)
    total = [g[-1] + mine(later)]
    g[-1] = g[-1] + mine(after)
    for i in range(SPAN - 2, -1, -1):
        total.insert(0, g[i] + c[i + 1] * total[0])
    smooth = mine(earlier)
    for i in range(SPAN):
        smooth = c[i] * smooth + (1.0 - c[i] * c[i]) * total[i]
        for e, value in enumerate((g[i], smooth)):
            first = (i * 2 + e) * SHARE
            out[first : first + SHARE, :] = value


def unpack_kernel(parts, gradient, direction):
    for e, out in enumerate((gradient, direction)):
        for f in range(FIELDS):
            half, odd = divmod(f, 2)
            for t in range(TILES):
                first = half * ROWS * 2 * SHARE + e * SHARE + odd * TILES + t
                out[f, :, t * LANE : (t + 1) * LANE] = parts[pl.ds(first, ROWS, stride=2 * SHARE), :]


def on_device(
    increments, correlation, coefficients, obs_cell, obs_value, obs_weight, obs_count, obs_step
):
    vmem = pl.BlockSpec(memory_space=pltpu.VMEM)
    far = pl.BlockSpec(memory_space=pltpu.HBM)
    limit = pltpu.CompilerParams(vmem_limit_bytes=32 * 1024 * 1024)
    mine = pl.pallas_call(
        pack_kernel,
        out_shape=jax.ShapeDtypeStruct((PACK, LON), jnp.float32),
        in_specs=[far] * 5 + [pl.BlockSpec(memory_space=pltpu.SMEM)],
        out_specs=vmem,
        scratch_shapes=[
            pltpu.VMEM((ROWS, LANE), jnp.int32),
            pltpu.VMEM((ROWS, LANE), jnp.float32),
            pltpu.SemaphoreType.DMA((5,)),
        ],
        compiler_params=pltpu.CompilerParams(vmem_limit_bytes=60 * 1024 * 1024),
    )(
        increments.reshape(FIELDS * ROWS, LON),
        coefficients.reshape(6 * ROWS, LON),
        obs_cell.reshape(ROWS, LANE),
        obs_value.reshape(ROWS, LANE),
        obs_weight.reshape(ROWS, LANE),
        obs_count,
    )
    packed = lax.all_gather(mine, "lat", axis=0, tiled=True)
    spans = [list(range(first, first + SPAN)) for first in range(0, TIMES, SPAN)]
    strides = [list(range(first, TIMES, SPAN)) for first in range(SPAN)]
    sent = pl.pallas_call(
        subwindow_kernel,
        out_shape=jax.ShapeDtypeStruct((SPAN * KINDS * SHARE, LANE), jnp.float32),
        in_specs=[vmem] * 3,
        out_specs=vmem,
        scratch_shapes=[pltpu.VMEM((FIELDS * WIN, LON), jnp.float32)],
        compiler_params=limit,
    )(obs_step.reshape(1, 1), packed, correlation[0])
    owned = lax.all_to_all(sent, "tm", 0, 0, axis_index_groups=spans, tiled=True)
    reduced = pl.pallas_call(
        block_kernel,
        out_shape=jax.ShapeDtypeStruct((BLOCKS * MAPS * SHARE, LANE), jnp.float32),
        in_specs=[vmem],
        out_specs=vmem,
        compiler_params=limit,
    )(owned)
    maps = lax.all_to_all(reduced, "tm", 0, 0, axis_index_groups=strides, tiled=True)
    solved = pl.pallas_call(
        time_kernel,
        out_shape=jax.ShapeDtypeStruct((SPAN * 2 * SHARE, LANE), jnp.float32),
        in_specs=[vmem] * 2,
        out_specs=vmem,
        compiler_params=limit,
    )(owned, maps)
    returned = lax.all_to_all(solved, "tm", 0, 0, axis_index_groups=spans, tiled=True)
    shape = jax.ShapeDtypeStruct((FIELDS, ROWS, LON), jnp.float32)
    gradient, direction = pl.pallas_call(
        unpack_kernel,
        out_shape=(shape, shape),
        in_specs=[vmem],
        out_specs=(vmem, vmem),
        compiler_params=limit,
    )(returned)
    return gradient[None], direction[None]


def solution(mesh):
    return jax.shard_map(
        on_device,
        mesh=mesh,
        in_specs=(
            P("tm", None, "lat", None),
            P("tm", None, "lat", None),
            P(None, "lat", None),
            P("tm", "lat"),
            P("tm", "lat"),
            P("tm", "lat"),
            P("tm", "lat"),
            P("tm"),
        ),
        out_specs=(P("tm", None, "lat", None), P("tm", None, "lat", None)),
        check_vma=False,
    )
```

```python
import jax
import jax.numpy as jnp
from jax import lax
from jax.experimental import pallas as pl
from jax.experimental.pallas import tpu as pltpu
from jax.sharding import PartitionSpec as P

STEPS = 4
FIELDS = 4
NY = 32
LON = 384
ROWS = 8
SLABS = 4
WIN = 3 * ROWS
MID = 16
LANE = 128
TILES = LON // LANE
PACK = 11 * ROWS
KINDS = 4
TIMES = 128
SPAN = 16
BLOCKS = TIMES // SPAN
SHARE = FIELDS * ROWS * TILES // SPAN
MAPS = 8
CHUNK = 512


def lon_roll(field, by):
    return pltpu.roll(field, by % LON, 1)


def row_roll(field, by):
    return pltpu.roll(field, by % field.shape[0], 0)


def step(state, coef, sign):
    h, u, v, q = state
    keep, kx, kw, ky, ks, cx, cw, cy, cs = coef["common"]
    qe, qw, qn, qs = coef["forward" if sign > 0 else "backward"]

    def sides(f):
        return lon_roll(f, -1), lon_roll(f, 1), row_roll(f, -1), row_roll(f, 1)

    def spread(f, e, w, n, s):
        return keep * f + (kx * e + kw * w) + (ky * n + ks * s)

    he, hw, hn, hs = sides(h)
    ue, uw, un, us = sides(u)
    ve, vw, vn, vs = sides(v)
    te, tw, tn, ts = sides(q)
    div = (cw * uw - cx * u) + (cs * vs - cy * v)
    gx = cx * (he - h)
    gy = cy * (hn - h)
    new_h = spread(h, he, hw, hn, hs)
    new_u = spread(u, ue, uw, un, us)
    new_v = spread(v, ve, vw, vn, vs)
    new_q = keep * q + (qe * te + qw * tw) + (qn * tn + qs * ts)
    if sign > 0:
        return new_h + div, new_u - gx, new_v - gy, new_q
    return new_h - div, new_u + gx, new_v + gy, new_q


def split(value):
    big = value.astype(jnp.bfloat16)
    return big, (value - big.astype(jnp.float32)).astype(jnp.bfloat16)


def pack_kernel(inc, coef, cell, value, weight, count, out, cell_buf, weight_buf, sems):
    first = (FIELDS + 6) * ROWS
    moves = (
        (cell, cell_buf),
        (weight, weight_buf),
        (coef, out.at[FIELDS * ROWS : first, :]),
        (inc, out.at[0 : FIELDS * ROWS, :]),
        (value, out.at[first:PACK, LANE : 2 * LANE]),
    )
    copies = [pltpu.make_async_copy(a, b, sems.at[i]) for i, (a, b) in enumerate(moves)]
    for copy in copies:
        copy.start()
    slot = lax.broadcasted_iota(jnp.int32, (ROWS, LANE), 0) * LANE
    slot = slot + lax.broadcasted_iota(jnp.int32, (ROWS, LANE), 1)
    live = slot < count[0, 0]
    for copy in copies[:2]:
        copy.wait()
    out[first:PACK, 0:LANE] = cell_buf[...].astype(jnp.float32)
    out[first:PACK, 2 * LANE :] = jnp.where(live, weight_buf[...], 0.0)
    for copy in copies[2:]:
        copy.wait()


def subwindow_kernel(obs_step, packed, rates, out):
    slab = lax.axis_index("lat")
    obs_at = jnp.broadcast_to(obs_step[...], (WIN, LON))

    def window(base):
        parts = []
        for offset in (-1, 0, 1):
            at = slab + offset
            inside = jnp.logical_and(at >= 0, at < SLABS)
            first = jnp.clip(at, 0, SLABS - 1) * PACK + base
            part = packed[pl.ds(pl.multiple_of(first, ROWS), ROWS), :]
            parts.append(jnp.where(inside, part, 0.0))
        return jnp.concatenate(parts, axis=0)

    row = lax.broadcasted_iota(jnp.int32, (WIN, LON), 0) + (slab - 1) * ROWS
    in_grid = jnp.logical_and(row >= 0, row < NY)
    inc = tuple(window(f * ROWS) for f in range(FIELDS))
    cx, cy, ax, by, kx, ky = (window((FIELDS + i) * ROWS) for i in range(6))

    def south(c):
        return jnp.where(in_grid, row_roll(c, 1), 0.0)

    kw, ks, cw, cs = lon_roll(kx, 1), south(ky), lon_roll(cx, 1), south(cy)
    aw, bs = lon_roll(ax, 1), south(by)
    keep = 1.0 - ((kx + kw) + (ky + ks))
    coef = {
        "common": (keep, kx, kw, ky, ks, cx, cw, cy, cs),
        "forward": (kx - ax, kw + aw, ky - by, ks + bs),
        "backward": (kx + ax, kw - aw, ky + by, ks - bs),
    }
    state = inc
    seen = inc
    for turn in range(STEPS):
        state = step(state, coef, 1.0)
        if turn == 0:
            seen = state
        else:
            seen = tuple(jnp.where(obs_at == turn + 1, a, b) for a, b in zip(state, seen, strict=True))
    end = state

    upper = lax.broadcasted_iota(jnp.int32, (ROWS, LON), 0) < ROWS // 2

    def fold(x):
        ends = jnp.where(upper, x[2 * ROWS :], x[:ROWS])
        return jnp.concatenate([x[ROWS : 2 * ROWS], ends], axis=0)

    inc, end, seen = (tuple(fold(x) for x in fields) for fields in (inc, end, seen))
    coef = {name: tuple(fold(x) for x in coef[name]) for name in ("common", "backward")}
    table = jnp.concatenate(
        [seen[f][:, t * LANE : (t + 1) * LANE] for t in range(TILES) for f in range(FIELDS)], axis=0
    )
    high = table.shape[0]
    table_parts = jnp.concatenate(split(jnp.transpose(table)), axis=0)

    half = jnp.bfloat16
    hi_iota = lax.broadcasted_iota(jnp.int32, (high, CHUNK), 0).astype(half)
    lo_iota = lax.broadcasted_iota(jnp.int32, (LANE, CHUNK), 0)
    lo_half = lo_iota.astype(half)
    one, none = jnp.ones((high, CHUNK), half), jnp.zeros((high, CHUNK), half)
    forcing = jnp.zeros((high, 2 * LANE), jnp.float32)
    for owner in range(SLABS):
        base = owner * PACK + 10 * ROWS
        cell = packed[base : base + ROWS, 0:LANE].astype(jnp.int32)
        value = packed[base : base + ROWS, LANE : 2 * LANE]
        weight = packed[base : base + ROWS, 2 * LANE : 3 * LANE]
        low = jnp.bitwise_and(cell, LANE - 1)
        tile_row = jnp.right_shift(cell, 7)
        field_row = jnp.right_shift(tile_row * 21846, 16)
        tile = tile_row - field_row * TILES
        field = jnp.right_shift(field_row, 5)
        rel = jnp.bitwise_and(field_row, NY - 1) - slab * ROWS
        near = jnp.logical_and(rel >= -(ROWS // 2), rel < ROWS + ROWS // 2)
        place = tile * (FIELDS * MID) + field * MID + jnp.bitwise_and(rel, MID - 1)
        spot = jnp.where(near, place, -1)
        for pair in range(ROWS // 4):
            rows = tuple(range(4 * pair, 4 * pair + 4))
            def wide(x):
                return jnp.concatenate([x[r : r + 1, :] for r in rows], axis=1)

            here, column = wide(spot), wide(low)
            pick = jnp.where(hi_iota == here.astype(half), one, none)
            match = lo_iota == column
            match_half = lo_half == column.astype(half)
            columns = lax.dot_general(
                table_parts, pick, (((1,), (0,)), ((), ())), preferred_element_type=jnp.float32
            )
            columns = columns[:LANE] + columns[LANE:]
            sampled = jnp.sum(jnp.where(match, columns, 0.0), axis=0, keepdims=True)
            depart = wide(weight) * (sampled - wide(value))
            big = depart.astype(half)
            small = (depart - big.astype(jnp.float32)).astype(half)
            placed = jnp.concatenate(
                [jnp.where(match_half, part, none[:LANE]) for part in (big, small)], axis=0
            )
            forcing = forcing + lax.dot_general(
                pick, placed, (((1,), (1,)), ((), ())), preferred_element_type=jnp.float32
            )
    forcing = forcing[:, :LANE] + forcing[:, LANE:]

    back = inc
    for _ in range(STEPS):
        back = step(back, coef, -1.0)

    inject = tuple(
        jnp.concatenate(
            [
                forcing[(t * FIELDS + f) * MID : (t * FIELDS + f + 1) * MID, :]
                for t in range(TILES)
            ],
            axis=1,
        )
        for f in range(FIELDS)
    )

    def push(state, turn):
        scale = jnp.where(obs_at[:MID] == turn, 1.0, 0.0)
        return tuple(a + scale * b for a, b in zip(state, inject, strict=True))

    follows = jnp.where(lax.axis_index("tm") < TIMES - 1, 1.0, 0.0)
    adjoint = push(tuple(follows * e for e in end), STEPS)
    for turn in range(STEPS):
        adjoint = push(step(adjoint, coef, -1.0), STEPS - 1 - turn)

    mine = slice(0, ROWS)
    for f in range(FIELDS):
        kinds = (inc[f][mine] + adjoint[f][mine], -end[f][mine], -back[f][mine], rates[f])
        half, odd = divmod(f, 2)
        for q, kind in enumerate(kinds):
            for t in range(TILES):
                first = half * ROWS * KINDS * SHARE + q * SHARE + odd * TILES + t
                out[pl.ds(first, ROWS, stride=KINDS * SHARE), :] = kind[:, t * LANE : (t + 1) * LANE]


def load_block(parts):
    def load(i, q):
        first = (i * KINDS + q) * SHARE
        return parts[first : first + SHARE, :]

    x, y, z, c = ([load(i, q) for i in range(SPAN)] for q in range(KINDS))
    g = list(x)
    for i in range(1, SPAN):
        g[i] = g[i] + y[i - 1]
        g[i - 1] = g[i - 1] + z[i]
    return g, y, z, c


def block_kernel(parts, out):
    g, y, z, c = load_block(parts)
    sums, factors = [g[-1]], [jnp.ones_like(g[-1])]
    for i in range(SPAN - 2, -1, -1):
        sums.insert(0, g[i] + c[i + 1] * sums[0])
        factors.insert(0, c[i + 1] * factors[0])
    shares = [1.0 - r * r for r in c]
    own, push = shares[0] * sums[0], shares[0] * factors[0]
    for i in range(1, SPAN):
        own = c[i] * own + shares[i] * sums[i]
        push = c[i] * push + shares[i] * factors[i]
    terms = (
        c[0] * factors[0],
        c[0],
        push,
        shares[0] * factors[0],
        c[0] * sums[0] + z[0],
        own,
        y[-1],
        z[0],
    )
    size = MAPS * SHARE
    for i, term in enumerate(terms):
        out[i * SHARE : (i + 1) * SHARE, :] = term
    whole = out[0:size, :]
    for b in range(1, BLOCKS):
        out[b * size : (b + 1) * size, :] = whole


def time_kernel(parts, maps, out):
    block = jnp.right_shift(lax.axis_index("tm"), 4)

    def term(b, i):
        first = (b * MAPS + i) * SHARE
        return maps[first : first + SHARE, :]

    through, first_rate, push, edge, back, own, last_y, first_z = (
        [term(b, i) for b in range(BLOCKS)] for i in range(MAPS)
    )
    zero = jnp.zeros_like(own[0])
    before = [zero] + last_y[:-1]
    after = first_z[1:] + [zero]
    later = [zero]
    for b in range(BLOCKS - 1, 0, -1):
        later.insert(0, (back[b] + first_rate[b] * before[b]) + through[b] * later[0])
    earlier = [zero]
    for b in range(BLOCKS - 1):
        made = (own[b] + push[b] * later[b]) + edge[b] * before[b]
        earlier.append(made + through[b] * earlier[-1])

    def mine(values):
        picked = values[0]
        for b in range(1, BLOCKS):
            picked = jnp.where(block == b, values[b], picked)
        return picked

    g, _, _, c = load_block(parts)
    g[0] = g[0] + mine(before)
    total = [g[-1] + mine(later)]
    g[-1] = g[-1] + mine(after)
    for i in range(SPAN - 2, -1, -1):
        total.insert(0, g[i] + c[i + 1] * total[0])
    smooth = mine(earlier)
    for i in range(SPAN):
        smooth = c[i] * smooth + (1.0 - c[i] * c[i]) * total[i]
        for e, value in enumerate((g[i], smooth)):
            first = (i * 2 + e) * SHARE
            out[first : first + SHARE, :] = value


def unpack_kernel(parts, gradient, direction):
    for e, out in enumerate((gradient, direction)):
        for f in range(FIELDS):
            half, odd = divmod(f, 2)
            for t in range(TILES):
                first = half * ROWS * 2 * SHARE + e * SHARE + odd * TILES + t
                out[f, :, t * LANE : (t + 1) * LANE] = parts[pl.ds(first, ROWS, stride=2 * SHARE), :]


def on_device(
    increments, correlation, coefficients, obs_cell, obs_value, obs_weight, obs_count, obs_step
):
    vmem = pl.BlockSpec(memory_space=pltpu.VMEM)
    far = pl.BlockSpec(memory_space=pltpu.HBM)
    limit = pltpu.CompilerParams(vmem_limit_bytes=32 * 1024 * 1024)
    mine = pl.pallas_call(
        pack_kernel,
        out_shape=jax.ShapeDtypeStruct((PACK, LON), jnp.float32),
        in_specs=[far] * 5 + [pl.BlockSpec(memory_space=pltpu.SMEM)],
        out_specs=vmem,
        scratch_shapes=[
            pltpu.VMEM((ROWS, LANE), jnp.int32),
            pltpu.VMEM((ROWS, LANE), jnp.float32),
            pltpu.SemaphoreType.DMA((5,)),
        ],
        compiler_params=pltpu.CompilerParams(vmem_limit_bytes=60 * 1024 * 1024),
    )(
        increments.reshape(FIELDS * ROWS, LON),
        coefficients.reshape(6 * ROWS, LON),
        obs_cell.reshape(ROWS, LANE),
        obs_value.reshape(ROWS, LANE),
        obs_weight.reshape(ROWS, LANE),
        obs_count,
    )
    packed = lax.all_gather(mine, "lat", axis=0, tiled=True)
    spans = [list(range(first, first + SPAN)) for first in range(0, TIMES, SPAN)]
    strides = [list(range(first, TIMES, SPAN)) for first in range(SPAN)]
    sent = pl.pallas_call(
        subwindow_kernel,
        out_shape=jax.ShapeDtypeStruct((SPAN * KINDS * SHARE, LANE), jnp.float32),
        in_specs=[vmem] * 3,
        out_specs=vmem,
        compiler_params=limit,
    )(obs_step.reshape(1, 1), packed, correlation[0])
    owned = lax.all_to_all(sent, "tm", 0, 0, axis_index_groups=spans, tiled=True)
    reduced = pl.pallas_call(
        block_kernel,
        out_shape=jax.ShapeDtypeStruct((BLOCKS * MAPS * SHARE, LANE), jnp.float32),
        in_specs=[vmem],
        out_specs=vmem,
        compiler_params=limit,
    )(owned)
    maps = lax.all_to_all(reduced, "tm", 0, 0, axis_index_groups=strides, tiled=True)
    solved = pl.pallas_call(
        time_kernel,
        out_shape=jax.ShapeDtypeStruct((SPAN * 2 * SHARE, LANE), jnp.float32),
        in_specs=[vmem] * 2,
        out_specs=vmem,
        compiler_params=limit,
    )(owned, maps)
    returned = lax.all_to_all(solved, "tm", 0, 0, axis_index_groups=spans, tiled=True)
    shape = jax.ShapeDtypeStruct((FIELDS, ROWS, LON), jnp.float32)
    gradient, direction = pl.pallas_call(
        unpack_kernel,
        out_shape=(shape, shape),
        in_specs=[vmem],
        out_specs=(vmem, vmem),
        compiler_params=limit,
    )(returned)
    return gradient[None], direction[None]


def solution(mesh):
    return jax.shard_map(
        on_device,
        mesh=mesh,
        in_specs=(
            P("tm", None, "lat", None),
            P("tm", None, "lat", None),
            P(None, "lat", None),
            P("tm", "lat"),
            P("tm", "lat"),
            P("tm", "lat"),
            P("tm", "lat"),
            P("tm"),
        ),
        out_specs=(P("tm", None, "lat", None), P("tm", None, "lat", None)),
        check_vma=False,
    )
```

```python
import jax
import jax.numpy as jnp
from jax import lax
from jax.experimental import pallas as pl
from jax.experimental.pallas import tpu as pltpu
from jax.sharding import PartitionSpec as P

STEPS = 4
FIELDS = 4
NY = 32
LON = 384
ROWS = 8
SLABS = 4
WIN = 3 * ROWS
MID = 16
LANE = 128
TILES = LON // LANE
PACK = 11 * ROWS
KINDS = 4
TIMES = 128
SPAN = 16
BLOCKS = TIMES // SPAN
SHARE = FIELDS * ROWS * TILES // SPAN
MAPS = 8
CHUNK = 512


def lon_roll(field, by):
    return pltpu.roll(field, by % LON, 1)


def row_roll(field, by):
    return pltpu.roll(field, by % field.shape[0], 0)


def step(state, coef, sign):
    h, u, v, q = state
    keep, kx, kw, ky, ks, cx, cw, cy, cs = coef["common"]
    qe, qw, qn, qs = coef["forward" if sign > 0 else "backward"]

    def sides(f):
        return lon_roll(f, -1), lon_roll(f, 1), row_roll(f, -1), row_roll(f, 1)

    def spread(f, e, w, n, s):
        return keep * f + (kx * e + kw * w) + (ky * n + ks * s)

    he, hw, hn, hs = sides(h)
    ue, uw, un, us = sides(u)
    ve, vw, vn, vs = sides(v)
    te, tw, tn, ts = sides(q)
    div = (cw * uw - cx * u) + (cs * vs - cy * v)
    gx = cx * (he - h)
    gy = cy * (hn - h)
    new_h = spread(h, he, hw, hn, hs)
    new_u = spread(u, ue, uw, un, us)
    new_v = spread(v, ve, vw, vn, vs)
    new_q = keep * q + (qe * te + qw * tw) + (qn * tn + qs * ts)
    if sign > 0:
        return new_h + div, new_u - gx, new_v - gy, new_q
    return new_h - div, new_u + gx, new_v + gy, new_q


def split(value):
    big = value.astype(jnp.bfloat16)
    return big, (value - big.astype(jnp.float32)).astype(jnp.bfloat16)


def pack_kernel(inc, coef, cell, value, weight, count, out, cell_buf, weight_buf, sems):
    first = (FIELDS + 6) * ROWS
    moves = (
        (cell, cell_buf),
        (weight, weight_buf),
        (coef, out.at[FIELDS * ROWS : first, :]),
        (inc, out.at[0 : FIELDS * ROWS, :]),
        (value, out.at[first:PACK, LANE : 2 * LANE]),
    )
    copies = [pltpu.make_async_copy(a, b, sems.at[i]) for i, (a, b) in enumerate(moves)]
    for copy in copies:
        copy.start()
    slot = lax.broadcasted_iota(jnp.int32, (ROWS, LANE), 0) * LANE
    slot = slot + lax.broadcasted_iota(jnp.int32, (ROWS, LANE), 1)
    live = slot < count[0, 0]
    for copy in copies[:2]:
        copy.wait()
    out[first:PACK, 0:LANE] = cell_buf[...].astype(jnp.float32)
    out[first:PACK, 2 * LANE :] = jnp.where(live, weight_buf[...], 0.0)
    for copy in copies[2:]:
        copy.wait()


def subwindow_kernel(obs_step, packed, rates, out):
    slab = lax.axis_index("lat")
    obs_at = jnp.broadcast_to(obs_step[...], (WIN, LON))

    def window(base):
        parts = []
        for offset in (-1, 0, 1):
            at = slab + offset
            inside = jnp.logical_and(at >= 0, at < SLABS)
            first = jnp.clip(at, 0, SLABS - 1) * PACK + base
            part = packed[pl.ds(pl.multiple_of(first, ROWS), ROWS), :]
            parts.append(jnp.where(inside, part, 0.0))
        return jnp.concatenate(parts, axis=0)

    row = lax.broadcasted_iota(jnp.int32, (WIN, LON), 0) + (slab - 1) * ROWS
    in_grid = jnp.logical_and(row >= 0, row < NY)
    inc = tuple(window(f * ROWS) for f in range(FIELDS))
    cx, cy, ax, by, kx, ky = (window((FIELDS + i) * ROWS) for i in range(6))

    def south(c):
        return jnp.where(in_grid, row_roll(c, 1), 0.0)

    kw, ks, cw, cs = lon_roll(kx, 1), south(ky), lon_roll(cx, 1), south(cy)
    aw, bs = lon_roll(ax, 1), south(by)
    keep = 1.0 - ((kx + kw) + (ky + ks))
    coef = {
        "common": (keep, kx, kw, ky, ks, cx, cw, cy, cs),
        "forward": (kx - ax, kw + aw, ky - by, ks + bs),
        "backward": (kx + ax, kw - aw, ky + by, ks - bs),
    }
    state = inc
    seen = inc
    for turn in range(STEPS):
        state = step(state, coef, 1.0)
        if turn == 0:
            seen = state
        else:
            seen = tuple(jnp.where(obs_at == turn + 1, a, b) for a, b in zip(state, seen, strict=True))
    end = state

    upper = lax.broadcasted_iota(jnp.int32, (ROWS, LON), 0) < ROWS // 2

    def fold(x):
        ends = jnp.where(upper, x[2 * ROWS :], x[:ROWS])
        return jnp.concatenate([x[ROWS : 2 * ROWS], ends], axis=0)

    inc, end, seen = (tuple(fold(x) for x in fields) for fields in (inc, end, seen))
    coef = {name: tuple(fold(x) for x in coef[name]) for name in ("common", "backward")}
    table = jnp.concatenate(
        [seen[f][:, t * LANE : (t + 1) * LANE] for t in range(TILES) for f in range(FIELDS)], axis=0
    )
    high = table.shape[0]
    table_parts = jnp.concatenate(split(jnp.transpose(table)), axis=0)

    half = jnp.bfloat16
    hi_iota = lax.broadcasted_iota(jnp.int32, (high, CHUNK), 0).astype(half)
    lo_iota = lax.broadcasted_iota(jnp.int32, (LANE, CHUNK), 0)
    lo_half = lo_iota.astype(half)
    one, none = jnp.ones((high, CHUNK), half), jnp.zeros((high, CHUNK), half)
    forcing = jnp.zeros((high, 2 * LANE), jnp.float32)
    for owner in range(SLABS):
        base = owner * PACK + 10 * ROWS
        cell = packed[base : base + ROWS, 0:LANE].astype(jnp.int32)
        value = packed[base : base + ROWS, LANE : 2 * LANE]
        weight = packed[base : base + ROWS, 2 * LANE : 3 * LANE]
        low = jnp.bitwise_and(cell, LANE - 1)
        tile_row = jnp.right_shift(cell, 7)
        field_row = jnp.right_shift(tile_row * 21846, 16)
        tile = tile_row - field_row * TILES
        field = jnp.right_shift(field_row, 5)
        rel = jnp.bitwise_and(field_row, NY - 1) - slab * ROWS
        near = jnp.logical_and(rel >= -(ROWS // 2), rel < ROWS + ROWS // 2)
        place = tile * (FIELDS * MID) + field * MID + jnp.bitwise_and(rel, MID - 1)
        spot = jnp.where(near, place, -1)
        for pair in range(ROWS // 4):
            rows = tuple(range(4 * pair, 4 * pair + 4))
            def wide(x):
                return jnp.concatenate([x[r : r + 1, :] for r in rows], axis=1)

            here, column = wide(spot), wide(low)
            pick = jnp.where(hi_iota == here.astype(half), one, none)
            match = lo_iota == column
            match_half = lo_half == column.astype(half)
            columns = lax.dot_general(
                table_parts, pick, (((1,), (0,)), ((), ())), preferred_element_type=jnp.float32
            )
            columns = columns[:LANE] + columns[LANE:]
            sampled = jnp.sum(jnp.where(match, columns, 0.0), axis=0, keepdims=True)
            depart = wide(weight) * (sampled - wide(value))
            big = depart.astype(half)
            small = (depart - big.astype(jnp.float32)).astype(half)
            placed = jnp.concatenate(
                [jnp.where(match_half, part, none[:LANE]) for part in (big, small)], axis=0
            )
            forcing = forcing + lax.dot_general(
                pick, placed, (((1,), (1,)), ((), ())), preferred_element_type=jnp.float32
            )
    forcing = forcing[:, :LANE] + forcing[:, LANE:]

    back = inc
    for _ in range(STEPS):
        back = step(back, coef, -1.0)

    inject = tuple(
        jnp.concatenate(
            [
                forcing[(t * FIELDS + f) * MID : (t * FIELDS + f + 1) * MID, :]
                for t in range(TILES)
            ],
            axis=1,
        )
        for f in range(FIELDS)
    )

    def push(state, turn):
        scale = jnp.where(obs_at[:MID] == turn, 1.0, 0.0)
        return tuple(a + scale * b for a, b in zip(state, inject, strict=True))

    follows = jnp.where(lax.axis_index("tm") < TIMES - 1, 1.0, 0.0)
    adjoint = push(tuple(follows * e for e in end), STEPS)
    for turn in range(STEPS):
        adjoint = push(step(adjoint, coef, -1.0), STEPS - 1 - turn)

    mine = slice(0, ROWS)
    for f in range(FIELDS):
        kinds = (inc[f][mine] + adjoint[f][mine], -end[f][mine], -back[f][mine], rates[f])
        half, odd = divmod(f, 2)
        for q, kind in enumerate(kinds):
            for t in range(TILES):
                first = half * ROWS * KINDS * SHARE + q * SHARE + odd * TILES + t
                out[pl.ds(first, ROWS, stride=KINDS * SHARE), :] = kind[:, t * LANE : (t + 1) * LANE]


def load_block(parts):
    def load(i, q):
        first = (i * KINDS + q) * SHARE
        return parts[first : first + SHARE, :]

    x, y, z, c = ([load(i, q) for i in range(SPAN)] for q in range(KINDS))
    g = list(x)
    for i in range(1, SPAN):
        g[i] = g[i] + y[i - 1]
        g[i - 1] = g[i - 1] + z[i]
    return g, y, z, c


def block_kernel(parts, out):
    g, y, z, c = load_block(parts)
    sums, factors = [g[-1]], [jnp.ones_like(g[-1])]
    for i in range(SPAN - 2, -1, -1):
        sums.insert(0, g[i] + c[i + 1] * sums[0])
        factors.insert(0, c[i + 1] * factors[0])
    shares = [1.0 - r * r for r in c]
    own, push = shares[0] * sums[0], shares[0] * factors[0]
    for i in range(1, SPAN):
        own = c[i] * own + shares[i] * sums[i]
        push = c[i] * push + shares[i] * factors[i]
    terms = (
        c[0] * factors[0],
        c[0],
        push,
        shares[0] * factors[0],
        c[0] * sums[0] + z[0],
        own,
        y[-1],
        z[0],
    )
    size = MAPS * SHARE
    for i, term in enumerate(terms):
        out[i * SHARE : (i + 1) * SHARE, :] = term
    whole = out[0:size, :]
    for b in range(1, BLOCKS):
        out[b * size : (b + 1) * size, :] = whole


def time_kernel(parts, maps, out):
    block = jnp.right_shift(lax.axis_index("tm"), 4)

    def term(b, i):
        first = (b * MAPS + i) * SHARE
        return maps[first : first + SHARE, :]

    through, first_rate, push, edge, back, own, last_y, first_z = (
        [term(b, i) for b in range(BLOCKS)] for i in range(MAPS)
    )
    zero = jnp.zeros_like(own[0])
    before = [zero] + last_y[:-1]
    after = first_z[1:] + [zero]
    later = [zero]
    for b in range(BLOCKS - 1, 0, -1):
        later.insert(0, (back[b] + first_rate[b] * before[b]) + through[b] * later[0])
    earlier = [zero]
    for b in range(BLOCKS - 1):
        made = (own[b] + push[b] * later[b]) + edge[b] * before[b]
        earlier.append(made + through[b] * earlier[-1])

    def mine(values):
        picked = values[0]
        for b in range(1, BLOCKS):
            picked = jnp.where(block == b, values[b], picked)
        return picked

    g, _, _, c = load_block(parts)
    g[0] = g[0] + mine(before)
    total = [g[-1] + mine(later)]
    g[-1] = g[-1] + mine(after)
    for i in range(SPAN - 2, -1, -1):
        total.insert(0, g[i] + c[i + 1] * total[0])
    smooth = mine(earlier)
    for i in range(SPAN):
        smooth = c[i] * smooth + (1.0 - c[i] * c[i]) * total[i]
        for e, value in enumerate((g[i], smooth)):
            first = (i * 2 + e) * SHARE
            out[first : first + SHARE, :] = value


def unpack_kernel(parts, gradient, direction):
    for e, out in enumerate((gradient, direction)):
        for f in range(FIELDS):
            half, odd = divmod(f, 2)
            for t in range(TILES):
                first = half * ROWS * 2 * SHARE + e * SHARE + odd * TILES + t
                out[f, :, t * LANE : (t + 1) * LANE] = parts[pl.ds(first, ROWS, stride=2 * SHARE), :]


def on_device(
    increments, correlation, coefficients, obs_cell, obs_value, obs_weight, obs_count, obs_step
):
    vmem = pl.BlockSpec(memory_space=pltpu.VMEM)
    far = pl.BlockSpec(memory_space=pltpu.HBM)
    limit = pltpu.CompilerParams(vmem_limit_bytes=32 * 1024 * 1024)
    mine = pl.pallas_call(
        pack_kernel,
        out_shape=jax.ShapeDtypeStruct((PACK, LON), jnp.float32),
        in_specs=[far] * 5 + [pl.BlockSpec(memory_space=pltpu.SMEM)],
        out_specs=vmem,
        scratch_shapes=[
            pltpu.VMEM((ROWS, LANE), jnp.int32),
            pltpu.VMEM((ROWS, LANE), jnp.float32),
            pltpu.SemaphoreType.DMA((5,)),
        ],
        compiler_params=limit,
    )(
        *(
            pltpu.with_memory_space_constraint(part, pltpu.HBM)
            for part in (
                increments.reshape(FIELDS * ROWS, LON),
                coefficients.reshape(6 * ROWS, LON),
                obs_cell.reshape(ROWS, LANE),
                obs_value.reshape(ROWS, LANE),
                obs_weight.reshape(ROWS, LANE),
            )
        ),
        obs_count,
    )
    packed = lax.all_gather(mine, "lat", axis=0, tiled=True)
    spans = [list(range(first, first + SPAN)) for first in range(0, TIMES, SPAN)]
    strides = [list(range(first, TIMES, SPAN)) for first in range(SPAN)]
    sent = pl.pallas_call(
        subwindow_kernel,
        out_shape=jax.ShapeDtypeStruct((SPAN * KINDS * SHARE, LANE), jnp.float32),
        in_specs=[vmem] * 3,
        out_specs=vmem,
        compiler_params=limit,
    )(obs_step.reshape(1, 1), packed, correlation[0])
    owned = lax.all_to_all(sent, "tm", 0, 0, axis_index_groups=spans, tiled=True)
    reduced = pl.pallas_call(
        block_kernel,
        out_shape=jax.ShapeDtypeStruct((BLOCKS * MAPS * SHARE, LANE), jnp.float32),
        in_specs=[vmem],
        out_specs=vmem,
        compiler_params=limit,
    )(owned)
    maps = lax.all_to_all(reduced, "tm", 0, 0, axis_index_groups=strides, tiled=True)
    solved = pl.pallas_call(
        time_kernel,
        out_shape=jax.ShapeDtypeStruct((SPAN * 2 * SHARE, LANE), jnp.float32),
        in_specs=[vmem] * 2,
        out_specs=vmem,
        compiler_params=limit,
    )(owned, maps)
    returned = lax.all_to_all(solved, "tm", 0, 0, axis_index_groups=spans, tiled=True)
    shape = jax.ShapeDtypeStruct((FIELDS, ROWS, LON), jnp.float32)
    gradient, direction = pl.pallas_call(
        unpack_kernel,
        out_shape=(shape, shape),
        in_specs=[vmem],
        out_specs=(vmem, vmem),
        compiler_params=limit,
    )(returned)
    return gradient[None], direction[None]


def solution(mesh):
    return jax.shard_map(
        on_device,
        mesh=mesh,
        in_specs=(
            P("tm", None, "lat", None),
            P("tm", None, "lat", None),
            P(None, "lat", None),
            P("tm", "lat"),
            P("tm", "lat"),
            P("tm", "lat"),
            P("tm", "lat"),
            P("tm"),
        ),
        out_specs=(P("tm", None, "lat", None), P("tm", None, "lat", None)),
        check_vma=False,
    )
```

```python
import jax
import jax.numpy as jnp
from jax import lax
from jax.experimental import pallas as pl
from jax.experimental.pallas import tpu as pltpu
from jax.sharding import PartitionSpec as P

STEPS = 4
FIELDS = 4
NY = 32
LON = 384
ROWS = 8
SLABS = 4
WIN = 3 * ROWS
MID = 16
LANE = 128
TILES = LON // LANE
PACK = 11 * ROWS
KINDS = 4
TIMES = 128
SPAN = 16
BLOCKS = TIMES // SPAN
SHARE = FIELDS * ROWS * TILES // SPAN
MAPS = 6
MAP_ROWS = MAPS * SHARE
CHUNK = 512


def lon_roll(field, by):
    return pltpu.roll(field, by % LON, 1)


def row_roll(field, by):
    return pltpu.roll(field, by % field.shape[0], 0)


def step(state, coef, sign):
    h, u, v, q = state
    keep, kx, kw, ky, ks, cx, cw, cy, cs = coef["common"]
    qe, qw, qn, qs = coef["forward" if sign > 0 else "backward"]

    def sides(f):
        return lon_roll(f, -1), lon_roll(f, 1), row_roll(f, -1), row_roll(f, 1)

    def spread(f, e, w, n, s):
        return keep * f + (kx * e + kw * w) + (ky * n + ks * s)

    he, hw, hn, hs = sides(h)
    ue, uw, un, us = sides(u)
    ve, vw, vn, vs = sides(v)
    te, tw, tn, ts = sides(q)
    div = (cw * uw - cx * u) + (cs * vs - cy * v)
    gx = cx * (he - h)
    gy = cy * (hn - h)
    new_h = spread(h, he, hw, hn, hs)
    new_u = spread(u, ue, uw, un, us)
    new_v = spread(v, ve, vw, vn, vs)
    new_q = keep * q + (qe * te + qw * tw) + (qn * tn + qs * ts)
    if sign > 0:
        return new_h + div, new_u - gx, new_v - gy, new_q
    return new_h - div, new_u + gx, new_v + gy, new_q


def split(value):
    big = value.astype(jnp.bfloat16)
    return big, (value - big.astype(jnp.float32)).astype(jnp.bfloat16)


def pack_kernel(inc, coef, cell, value, weight, count, out, cell_buf, weight_buf, sems):
    first = (FIELDS + 6) * ROWS
    moves = (
        (cell, cell_buf),
        (weight, weight_buf),
        (coef, out.at[FIELDS * ROWS : first, :]),
        (inc, out.at[0 : FIELDS * ROWS, :]),
        (value, out.at[first:PACK, LANE : 2 * LANE]),
    )
    copies = [pltpu.make_async_copy(a, b, sems.at[i]) for i, (a, b) in enumerate(moves)]
    for copy in copies:
        copy.start()
    slot = lax.broadcasted_iota(jnp.int32, (ROWS, LANE), 0) * LANE
    slot = slot + lax.broadcasted_iota(jnp.int32, (ROWS, LANE), 1)
    live = slot < count[0, 0]
    for copy in copies[:2]:
        copy.wait()
    out[first:PACK, 0:LANE] = cell_buf[...].astype(jnp.float32)
    out[first:PACK, 2 * LANE :] = jnp.where(live, weight_buf[...], 0.0)
    for copy in copies[2:]:
        copy.wait()


def subwindow_kernel(obs_step, packed, rates, out):
    slab = lax.axis_index("lat")
    obs_at = jnp.broadcast_to(obs_step[...], (WIN, LON))

    def window(base):
        parts = []
        for offset in (-1, 0, 1):
            at = slab + offset
            inside = jnp.logical_and(at >= 0, at < SLABS)
            first = jnp.clip(at, 0, SLABS - 1) * PACK + base
            part = packed[pl.ds(pl.multiple_of(first, ROWS), ROWS), :]
            parts.append(jnp.where(inside, part, 0.0))
        return jnp.concatenate(parts, axis=0)

    row = lax.broadcasted_iota(jnp.int32, (WIN, LON), 0) + (slab - 1) * ROWS
    in_grid = jnp.logical_and(row >= 0, row < NY)
    inc = tuple(window(f * ROWS) for f in range(FIELDS))
    cx, cy, ax, by, kx, ky = (window((FIELDS + i) * ROWS) for i in range(6))

    def south(c):
        return jnp.where(in_grid, row_roll(c, 1), 0.0)

    kw, ks, cw, cs = lon_roll(kx, 1), south(ky), lon_roll(cx, 1), south(cy)
    aw, bs = lon_roll(ax, 1), south(by)
    keep = 1.0 - ((kx + kw) + (ky + ks))
    coef = {
        "common": (keep, kx, kw, ky, ks, cx, cw, cy, cs),
        "forward": (kx - ax, kw + aw, ky - by, ks + bs),
        "backward": (kx + ax, kw - aw, ky + by, ks - bs),
    }
    state = inc
    seen = inc
    for turn in range(STEPS):
        state = step(state, coef, 1.0)
        if turn == 0:
            seen = state
        else:
            seen = tuple(jnp.where(obs_at == turn + 1, a, b) for a, b in zip(state, seen, strict=True))
    end = state

    upper = lax.broadcasted_iota(jnp.int32, (ROWS, LON), 0) < ROWS // 2

    def fold(x):
        ends = jnp.where(upper, x[2 * ROWS :], x[:ROWS])
        return jnp.concatenate([x[ROWS : 2 * ROWS], ends], axis=0)

    inc, end, seen = (tuple(fold(x) for x in fields) for fields in (inc, end, seen))
    coef = {name: tuple(fold(x) for x in coef[name]) for name in ("common", "backward")}
    table = jnp.concatenate(
        [seen[f][:, t * LANE : (t + 1) * LANE] for t in range(TILES) for f in range(FIELDS)], axis=0
    )
    high = table.shape[0]
    table_parts = jnp.concatenate(split(jnp.transpose(table)), axis=0)

    half = jnp.bfloat16
    hi_iota = lax.broadcasted_iota(jnp.int32, (high, CHUNK), 0).astype(half)
    lo_iota = lax.broadcasted_iota(jnp.int32, (LANE, CHUNK), 0)
    lo_half = lo_iota.astype(half)
    one, none = jnp.ones((high, CHUNK), half), jnp.zeros((high, CHUNK), half)
    picks, places = [], []
    for owner in range(SLABS):
        base = owner * PACK + 10 * ROWS
        cell = packed[base : base + ROWS, 0:LANE].astype(jnp.int32)
        value = packed[base : base + ROWS, LANE : 2 * LANE]
        weight = packed[base : base + ROWS, 2 * LANE : 3 * LANE]
        low = jnp.bitwise_and(cell, LANE - 1)
        tile_row = jnp.right_shift(cell, 7)
        field_row = jnp.right_shift(tile_row * 21846, 16)
        tile = tile_row - field_row * TILES
        field = jnp.right_shift(field_row, 5)
        rel = jnp.bitwise_and(field_row, NY - 1) - slab * ROWS
        near = jnp.logical_and(rel >= -(ROWS // 2), rel < ROWS + ROWS // 2)
        place = tile * (FIELDS * MID) + field * MID + jnp.bitwise_and(rel, MID - 1)
        spot = jnp.where(near, place, -1)
        for pair in range(ROWS // 4):
            rows = tuple(range(4 * pair, 4 * pair + 4))
            def wide(x):
                return jnp.concatenate([x[r : r + 1, :] for r in rows], axis=1)

            here, column = wide(spot), wide(low)
            pick = jnp.where(hi_iota == here.astype(half), one, none)
            match = lo_iota == column
            match_half = lo_half == column.astype(half)
            columns = lax.dot_general(
                table_parts, pick, (((1,), (0,)), ((), ())), preferred_element_type=jnp.float32
            )
            columns = columns[:LANE] + columns[LANE:]
            sampled = jnp.sum(jnp.where(match, columns, 0.0), axis=0, keepdims=True)
            depart = wide(weight) * (sampled - wide(value))
            big = depart.astype(half)
            small = (depart - big.astype(jnp.float32)).astype(half)
            placed = jnp.concatenate(
                [jnp.where(match_half, part, none[:LANE]) for part in (big, small)], axis=0
            )
            picks.append(pick)
            places.append(placed)
    forcing = lax.dot_general(
        jnp.concatenate(picks, axis=1),
        jnp.concatenate(places, axis=1),
        (((1,), (1,)), ((), ())),
        preferred_element_type=jnp.float32,
    )
    forcing = forcing[:, :LANE] + forcing[:, LANE:]

    back = inc
    for _ in range(STEPS):
        back = step(back, coef, -1.0)

    inject = tuple(
        jnp.concatenate(
            [
                forcing[(t * FIELDS + f) * MID : (t * FIELDS + f + 1) * MID, :]
                for t in range(TILES)
            ],
            axis=1,
        )
        for f in range(FIELDS)
    )

    def push(state, turn):
        scale = jnp.where(obs_at[:MID] == turn, 1.0, 0.0)
        return tuple(a + scale * b for a, b in zip(state, inject, strict=True))

    follows = jnp.where(lax.axis_index("tm") < TIMES - 1, 1.0, 0.0)
    adjoint = push(tuple(follows * e for e in end), STEPS)
    for turn in range(STEPS):
        adjoint = push(step(adjoint, coef, -1.0), STEPS - 1 - turn)

    mine = slice(0, ROWS)
    for f in range(FIELDS):
        kinds = (inc[f][mine] + adjoint[f][mine], -end[f][mine], -back[f][mine], rates[f])
        half, odd = divmod(f, 2)
        for q, kind in enumerate(kinds):
            for t in range(TILES):
                first = half * ROWS * KINDS * SHARE + q * SHARE + odd * TILES + t
                out[pl.ds(first, ROWS, stride=KINDS * SHARE), :] = kind[:, t * LANE : (t + 1) * LANE]


def load_block(parts):
    def load(i, q):
        first = (i * KINDS + q) * SHARE
        return parts[first : first + SHARE, :]

    x, y, z, c = ([load(i, q) for i in range(SPAN)] for q in range(KINDS))
    g = list(x)
    for i in range(1, SPAN):
        g[i] = g[i] + y[i - 1]
        g[i - 1] = g[i - 1] + z[i]
    return g, y, z, c


def block_kernel(parts, out):
    g, y, z, c = load_block(parts)
    sums, factors = [g[-1]], [jnp.ones_like(g[-1])]
    for i in range(SPAN - 2, -1, -1):
        sums.insert(0, g[i] + c[i + 1] * sums[0])
        factors.insert(0, c[i + 1] * factors[0])
    shares = [1.0 - r * r for r in c]
    own, push = shares[0] * sums[0], shares[0] * factors[0]
    for i in range(1, SPAN):
        own = c[i] * own + shares[i] * sums[i]
        push = c[i] * push + shares[i] * factors[i]
    block = jnp.right_shift(lax.axis_index("tm"), 4)
    terms = (factors[0], c[0], c[0] * sums[0] + z[0], y[-1], push, own)
    for i, term in enumerate(terms):
        out[i * SHARE : (i + 1) * SHARE, :] = term
    whole = out[0:MAP_ROWS, :]
    for b in range(BLOCKS):
        first = b * MAP_ROWS
        if b > 0:
            out[first : first + MAP_ROWS, :] = whole
        first += 4 * SHARE
        out[first : first + SHARE, :] = jnp.where(b < block, z[0], push)


def time_kernel(parts, maps, out):
    block = jnp.right_shift(lax.axis_index("tm"), 4)

    def term(b, i):
        first = b * MAP_ROWS + i * SHARE
        return maps[first : first + SHARE, :]

    factor, first_rate, back, last_y, shared, own = (
        [term(b, i) for b in range(BLOCKS)] for i in range(MAPS)
    )
    through = [r * f for r, f in zip(first_rate, factor, strict=True)]
    edge = [(1.0 - r * r) * f for r, f in zip(first_rate, factor, strict=True)]
    zero = jnp.zeros_like(own[0])
    before = [zero] + last_y[:-1]
    after = shared[1:] + [zero]
    later = [zero]
    for b in range(BLOCKS - 1, 0, -1):
        later.insert(0, (back[b] + first_rate[b] * before[b]) + through[b] * later[0])
    earlier = [zero]
    for b in range(BLOCKS - 1):
        made = (own[b] + shared[b] * later[b]) + edge[b] * before[b]
        earlier.append(made + through[b] * earlier[-1])

    def mine(values):
        picked = values[0]
        for b in range(1, BLOCKS):
            picked = jnp.where(block == b, values[b], picked)
        return picked

    g, _, _, c = load_block(parts)
    g[0] = g[0] + mine(before)
    total = [g[-1] + mine(later)]
    g[-1] = g[-1] + mine(after)
    for i in range(SPAN - 2, -1, -1):
        total.insert(0, g[i] + c[i + 1] * total[0])
    smooth = mine(earlier)
    for i in range(SPAN):
        smooth = c[i] * smooth + (1.0 - c[i] * c[i]) * total[i]
        for e, value in enumerate((g[i], smooth)):
            first = (i * 2 + e) * SHARE
            out[first : first + SHARE, :] = value


def unpack_kernel(parts, gradient, direction):
    for e, out in enumerate((gradient, direction)):
        for f in range(FIELDS):
            half, odd = divmod(f, 2)
            for t in range(TILES):
                first = half * ROWS * 2 * SHARE + e * SHARE + odd * TILES + t
                out[f, :, t * LANE : (t + 1) * LANE] = parts[pl.ds(first, ROWS, stride=2 * SHARE), :]


def on_device(
    increments, correlation, coefficients, obs_cell, obs_value, obs_weight, obs_count, obs_step
):
    vmem = pl.BlockSpec(memory_space=pltpu.VMEM)
    far = pl.BlockSpec(memory_space=pltpu.HBM)
    limit = pltpu.CompilerParams(vmem_limit_bytes=32 * 1024 * 1024)
    mine = pl.pallas_call(
        pack_kernel,
        out_shape=jax.ShapeDtypeStruct((PACK, LON), jnp.float32),
        in_specs=[far] * 5 + [pl.BlockSpec(memory_space=pltpu.SMEM)],
        out_specs=vmem,
        scratch_shapes=[
            pltpu.VMEM((ROWS, LANE), jnp.int32),
            pltpu.VMEM((ROWS, LANE), jnp.float32),
            pltpu.SemaphoreType.DMA((5,)),
        ],
        compiler_params=limit,
    )(
        *(
            pltpu.with_memory_space_constraint(part, pltpu.HBM)
            for part in (
                increments.reshape(FIELDS * ROWS, LON),
                coefficients.reshape(6 * ROWS, LON),
                obs_cell.reshape(ROWS, LANE),
                obs_value.reshape(ROWS, LANE),
                obs_weight.reshape(ROWS, LANE),
            )
        ),
        obs_count,
    )
    packed = lax.all_gather(mine, "lat", axis=0, tiled=True)
    spans = [list(range(first, first + SPAN)) for first in range(0, TIMES, SPAN)]
    strides = [list(range(first, TIMES, SPAN)) for first in range(SPAN)]
    sent = pl.pallas_call(
        subwindow_kernel,
        out_shape=jax.ShapeDtypeStruct((SPAN * KINDS * SHARE, LANE), jnp.float32),
        in_specs=[vmem] * 3,
        out_specs=vmem,
        compiler_params=limit,
    )(obs_step.reshape(1, 1), packed, correlation[0])
    owned = lax.all_to_all(sent, "tm", 0, 0, axis_index_groups=spans, tiled=True)
    reduced = pl.pallas_call(
        block_kernel,
        out_shape=jax.ShapeDtypeStruct((BLOCKS * MAP_ROWS, LANE), jnp.float32),
        in_specs=[vmem],
        out_specs=vmem,
        compiler_params=limit,
    )(owned)
    quarters = reduced.reshape(BLOCKS, -1, 4, LANE)
    maps = lax.all_to_all(quarters, "tm", 0, 0, axis_index_groups=strides, tiled=True)
    solved = pl.pallas_call(
        time_kernel,
        out_shape=jax.ShapeDtypeStruct((SPAN * 2 * SHARE, LANE), jnp.float32),
        in_specs=[vmem] * 2,
        out_specs=vmem,
        compiler_params=limit,
    )(owned, maps.reshape(BLOCKS * MAP_ROWS, LANE))
    quarters = solved.reshape(SPAN, -1, 4, LANE)
    returned = lax.all_to_all(quarters, "tm", 0, 0, axis_index_groups=spans, tiled=True)
    shape = jax.ShapeDtypeStruct((FIELDS, ROWS, LON), jnp.float32)
    gradient, direction = pl.pallas_call(
        unpack_kernel,
        out_shape=(shape, shape),
        in_specs=[vmem],
        out_specs=(vmem, vmem),
        compiler_params=limit,
    )(returned.reshape(SPAN * 2 * SHARE, LANE))
    return gradient[None], direction[None]


def solution(mesh):
    return jax.shard_map(
        on_device,
        mesh=mesh,
        in_specs=(
            P("tm", None, "lat", None),
            P("tm", None, "lat", None),
            P(None, "lat", None),
            P("tm", "lat"),
            P("tm", "lat"),
            P("tm", "lat"),
            P("tm", "lat"),
            P("tm"),
        ),
        out_specs=(P("tm", None, "lat", None), P("tm", None, "lat", None)),
        check_vma=False,
    )
```

```python
import jax
import jax.numpy as jnp
from jax import lax
from jax.experimental import pallas as pl
from jax.experimental.pallas import tpu as pltpu
from jax.sharding import PartitionSpec as P

STEPS = 4
FIELDS = 4
NY = 32
LON = 384
ROWS = 8
SLABS = 4
WIN = 3 * ROWS
MID = 16
LANE = 128
TILES = LON // LANE
PACK = 11 * ROWS
KINDS = 4
TIMES = 128
SPAN = 16
BLOCKS = TIMES // SPAN
SHARE = FIELDS * ROWS * TILES // SPAN
MAPS = 6
MAP_ROWS = MAPS * SHARE
CHUNK = 512
PARTS = ROWS * LANE // CHUNK


def lon_roll(field, by):
    return pltpu.roll(field, by % LON, 1)


def row_roll(field, by):
    return pltpu.roll(field, by % field.shape[0], 0)


def step(state, coef, sign):
    h, u, v, q = state
    keep, kx, kw, ky, ks, cx, cw, cy, cs = coef["common"]
    qe, qw, qn, qs = coef["forward" if sign > 0 else "backward"]

    def sides(f):
        return lon_roll(f, -1), lon_roll(f, 1), row_roll(f, -1), row_roll(f, 1)

    def spread(f, e, w, n, s):
        return keep * f + (kx * e + kw * w) + (ky * n + ks * s)

    he, hw, hn, hs = sides(h)
    ue, uw, un, us = sides(u)
    ve, vw, vn, vs = sides(v)
    te, tw, tn, ts = sides(q)
    div = (cw * uw - cx * u) + (cs * vs - cy * v)
    gx = cx * (he - h)
    gy = cy * (hn - h)
    new_h = spread(h, he, hw, hn, hs)
    new_u = spread(u, ue, uw, un, us)
    new_v = spread(v, ve, vw, vn, vs)
    new_q = keep * q + (qe * te + qw * tw) + (qn * tn + qs * ts)
    if sign > 0:
        return new_h + div, new_u - gx, new_v - gy, new_q
    return new_h - div, new_u + gx, new_v + gy, new_q


def split(value):
    big = value.astype(jnp.bfloat16)
    return big, (value - big.astype(jnp.float32)).astype(jnp.bfloat16)


def pack_kernel(inc, coef, cell, value, weight, count, out, cell_buf, weight_buf, sems):
    first = (FIELDS + 6) * ROWS
    moves = (
        (cell, cell_buf),
        (weight, weight_buf),
        (coef, out.at[FIELDS * ROWS : first, :]),
        (inc, out.at[0 : FIELDS * ROWS, :]),
        (value, out.at[first:PACK, LANE : 2 * LANE]),
    )
    copies = [pltpu.make_async_copy(a, b, sems.at[i]) for i, (a, b) in enumerate(moves)]
    for copy in copies:
        copy.start()
    slot = lax.broadcasted_iota(jnp.int32, (ROWS, LANE), 0) * LANE
    slot = slot + lax.broadcasted_iota(jnp.int32, (ROWS, LANE), 1)
    live = slot < count[0, 0]
    for copy in copies[:2]:
        copy.wait()
    out[first:PACK, 0:LANE] = cell_buf[...].astype(jnp.float32)
    out[first:PACK, 2 * LANE :] = jnp.where(live, weight_buf[...], 0.0)
    for copy in copies[2:]:
        copy.wait()


def subwindow_kernel(obs_step, packed, rates, out, picks):
    slab = lax.axis_index("lat")
    obs_at = obs_step[0]

    def window(base):
        parts = []
        for offset in (-1, 0, 1):
            at = slab + offset
            inside = jnp.logical_and(at >= 0, at < SLABS)
            first = jnp.clip(at, 0, SLABS - 1) * PACK + base
            part = packed[pl.ds(pl.multiple_of(first, ROWS), ROWS), :]
            parts.append(jnp.where(inside, part, 0.0))
        return jnp.concatenate(parts, axis=0)

    row = lax.broadcasted_iota(jnp.int32, (WIN, LON), 0) + (slab - 1) * ROWS
    in_grid = jnp.logical_and(row >= 0, row < NY)
    inc = tuple(window(f * ROWS) for f in range(FIELDS))
    cx, cy, ax, by, kx, ky = (window((FIELDS + i) * ROWS) for i in range(6))

    def south(c):
        return jnp.where(in_grid, row_roll(c, 1), 0.0)

    kw, ks, cw, cs = lon_roll(kx, 1), south(ky), lon_roll(cx, 1), south(cy)
    aw, bs = lon_roll(ax, 1), south(by)
    keep = 1.0 - ((kx + kw) + (ky + ks))
    coef = {
        "common": (keep, kx, kw, ky, ks, cx, cw, cy, cs),
        "forward": (kx - ax, kw + aw, ky - by, ks + bs),
        "backward": (kx + ax, kw - aw, ky + by, ks - bs),
    }
    high = FIELDS * MID * TILES
    half = jnp.bfloat16
    hi_iota = lax.broadcasted_iota(jnp.int32, (high, CHUNK), 0).astype(half)
    one, none = jnp.ones((high, CHUNK), half), jnp.zeros((high, CHUNK), half)

    def wide(x, part):
        first = part * (CHUNK // LANE)
        rows = range(first, first + CHUNK // LANE)
        return jnp.concatenate([x[r : r + 1, :] for r in rows], axis=1)

    def choose(owner):
        base = owner * PACK + 10 * ROWS
        cell = packed[base : base + ROWS, 0:LANE].astype(jnp.int32)
        tile_row = jnp.right_shift(cell, 7)
        field_row = jnp.right_shift(tile_row * 21846, 16)
        tile = tile_row - field_row * TILES
        field = jnp.right_shift(field_row, 5)
        rel = jnp.bitwise_and(field_row, NY - 1) - slab * ROWS
        near = jnp.logical_and(rel >= -(ROWS // 2), rel < ROWS + ROWS // 2)
        place = tile * (FIELDS * MID) + field * MID + jnp.bitwise_and(rel, MID - 1)
        spot = jnp.where(near, place, -1)
        for part in range(PARTS):
            at = (owner * PARTS + part) * CHUNK
            here = wide(spot, part).astype(half)
            picks[:, at : at + CHUNK] = jnp.where(hi_iota == here, one, none)
        return jnp.bitwise_and(cell, LANE - 1)

    lows = []
    state = inc
    seen = inc
    for turn in range(STEPS):
        state = step(state, coef, 1.0)
        lows.append(choose(turn))
        if turn == 0:
            seen = state
        else:
            seen = tuple(jnp.where(obs_at == turn + 1, a, b) for a, b in zip(state, seen, strict=True))
    end = state

    upper = lax.broadcasted_iota(jnp.int32, (ROWS, LON), 0) < ROWS // 2

    def fold(x):
        ends = jnp.where(upper, x[2 * ROWS :], x[:ROWS])
        return jnp.concatenate([x[ROWS : 2 * ROWS], ends], axis=0)

    inc, end, seen = (tuple(fold(x) for x in fields) for fields in (inc, end, seen))
    coef = {name: tuple(fold(x) for x in coef[name]) for name in ("common", "backward")}
    table = jnp.concatenate(
        [seen[f][:, t * LANE : (t + 1) * LANE] for t in range(TILES) for f in range(FIELDS)], axis=0
    )
    table_parts = jnp.concatenate(split(jnp.transpose(table)), axis=0)

    lo_iota = lax.broadcasted_iota(jnp.int32, (LANE, CHUNK), 0)
    lo_half = lo_iota.astype(half)
    places = []
    for owner in range(SLABS):
        base = owner * PACK + 10 * ROWS
        value = packed[base : base + ROWS, LANE : 2 * LANE]
        weight = packed[base : base + ROWS, 2 * LANE : 3 * LANE]
        for part in range(PARTS):
            at = (owner * PARTS + part) * CHUNK
            column = wide(lows[owner], part)
            columns = lax.dot_general(
                table_parts,
                picks[:, at : at + CHUNK],
                (((1,), (0,)), ((), ())),
                preferred_element_type=jnp.float32,
            )
            columns = columns[:LANE] + columns[LANE:]
            here = jnp.where(lo_iota == column, columns, 0.0)
            sampled = jnp.sum(here, axis=0, keepdims=True)
            depart = wide(weight, part) * (sampled - wide(value, part))
            big = depart.astype(half)
            small = (depart - big.astype(jnp.float32)).astype(half)
            match = lo_half == column.astype(half)
            places.append(
                jnp.concatenate(
                    [jnp.where(match, piece, none[:LANE]) for piece in (big, small)], axis=0
                )
            )
    forcing = lax.dot_general(
        picks[...],
        jnp.concatenate(places, axis=1),
        (((1,), (1,)), ((), ())),
        preferred_element_type=jnp.float32,
    )
    forcing = forcing[:, :LANE] + forcing[:, LANE:]

    back = inc
    for _ in range(STEPS):
        back = step(back, coef, -1.0)

    inject = tuple(
        jnp.concatenate(
            [
                forcing[(t * FIELDS + f) * MID : (t * FIELDS + f + 1) * MID, :]
                for t in range(TILES)
            ],
            axis=1,
        )
        for f in range(FIELDS)
    )

    def push(state, turn):
        scale = jnp.where(obs_at == turn, 1.0, 0.0)
        return tuple(a + scale * b for a, b in zip(state, inject, strict=True))

    follows = jnp.where(lax.axis_index("tm") < TIMES - 1, 1.0, 0.0)
    adjoint = push(tuple(follows * e for e in end), STEPS)
    for turn in range(STEPS):
        adjoint = push(step(adjoint, coef, -1.0), STEPS - 1 - turn)

    mine = slice(0, ROWS)
    for f in range(FIELDS):
        kinds = (inc[f][mine] + adjoint[f][mine], -end[f][mine], -back[f][mine], rates[f])
        half, odd = divmod(f, 2)
        for q, kind in enumerate(kinds):
            for t in range(TILES):
                first = half * ROWS * KINDS * SHARE + q * SHARE + odd * TILES + t
                out[pl.ds(first, ROWS, stride=KINDS * SHARE), :] = kind[:, t * LANE : (t + 1) * LANE]


def load_block(parts):
    def load(i, q):
        first = (i * KINDS + q) * SHARE
        return parts[first : first + SHARE, :]

    x, y, z, c = ([load(i, q) for i in range(SPAN)] for q in range(KINDS))
    g = list(x)
    for i in range(1, SPAN):
        g[i] = g[i] + y[i - 1]
        g[i - 1] = g[i - 1] + z[i]
    return g, y, z, c


def block_kernel(parts, out):
    g, y, z, c = load_block(parts)
    sums, factors = [g[-1]], [jnp.ones_like(g[-1])]
    for i in range(SPAN - 2, -1, -1):
        sums.insert(0, g[i] + c[i + 1] * sums[0])
        factors.insert(0, c[i + 1] * factors[0])
    shares = [1.0 - r * r for r in c]
    own, push = shares[0] * sums[0], shares[0] * factors[0]
    for i in range(1, SPAN):
        own = c[i] * own + shares[i] * sums[i]
        push = c[i] * push + shares[i] * factors[i]
    block = jnp.right_shift(lax.axis_index("tm"), 4)
    terms = (factors[0], c[0], c[0] * sums[0] + z[0], y[-1], push, own)
    for i, term in enumerate(terms):
        out[i * SHARE : (i + 1) * SHARE, :] = term
    whole = out[0:MAP_ROWS, :]
    for b in range(BLOCKS):
        first = b * MAP_ROWS
        if b > 0:
            out[first : first + MAP_ROWS, :] = whole
        first += 4 * SHARE
        out[first : first + SHARE, :] = jnp.where(b < block, z[0], push)


def time_kernel(parts, maps, out):
    block = jnp.right_shift(lax.axis_index("tm"), 4)

    def term(b, i):
        first = b * MAP_ROWS + i * SHARE
        return maps[first : first + SHARE, :]

    factor, first_rate, back, last_y, shared, own = (
        [term(b, i) for b in range(BLOCKS)] for i in range(MAPS)
    )
    through = [r * f for r, f in zip(first_rate, factor, strict=True)]
    edge = [(1.0 - r * r) * f for r, f in zip(first_rate, factor, strict=True)]
    zero = jnp.zeros_like(own[0])
    before = [zero] + last_y[:-1]
    after = shared[1:] + [zero]
    later = [zero]
    for b in range(BLOCKS - 1, 0, -1):
        later.insert(0, (back[b] + first_rate[b] * before[b]) + through[b] * later[0])
    earlier = [zero]
    for b in range(BLOCKS - 1):
        made = (own[b] + shared[b] * later[b]) + edge[b] * before[b]
        earlier.append(made + through[b] * earlier[-1])

    def mine(values):
        picked = values[0]
        for b in range(1, BLOCKS):
            picked = jnp.where(block == b, values[b], picked)
        return picked

    g, _, _, c = load_block(parts)
    g[0] = g[0] + mine(before)
    total = [g[-1] + mine(later)]
    g[-1] = g[-1] + mine(after)
    for i in range(SPAN - 2, -1, -1):
        total.insert(0, g[i] + c[i + 1] * total[0])
    smooth = mine(earlier)
    for i in range(SPAN):
        smooth = c[i] * smooth + (1.0 - c[i] * c[i]) * total[i]
        for e, value in enumerate((g[i], smooth)):
            first = (i * 2 + e) * SHARE
            out[first : first + SHARE, :] = value


def unpack_kernel(parts, gradient, direction):
    for e, out in enumerate((gradient, direction)):
        for f in range(FIELDS):
            half, odd = divmod(f, 2)
            for t in range(TILES):
                first = half * ROWS * 2 * SHARE + e * SHARE + odd * TILES + t
                out[f, :, t * LANE : (t + 1) * LANE] = parts[pl.ds(first, ROWS, stride=2 * SHARE), :]


def on_device(
    increments, correlation, coefficients, obs_cell, obs_value, obs_weight, obs_count, obs_step
):
    vmem = pl.BlockSpec(memory_space=pltpu.VMEM)
    far = pl.BlockSpec(memory_space=pltpu.HBM)
    limit = pltpu.CompilerParams(vmem_limit_bytes=32 * 1024 * 1024)
    mine = pl.pallas_call(
        pack_kernel,
        out_shape=jax.ShapeDtypeStruct((PACK, LON), jnp.float32),
        in_specs=[far] * 5 + [pl.BlockSpec(memory_space=pltpu.SMEM)],
        out_specs=vmem,
        scratch_shapes=[
            pltpu.VMEM((ROWS, LANE), jnp.int32),
            pltpu.VMEM((ROWS, LANE), jnp.float32),
            pltpu.SemaphoreType.DMA((5,)),
        ],
        compiler_params=limit,
    )(
        *(
            pltpu.with_memory_space_constraint(part, pltpu.HBM)
            for part in (
                increments.reshape(FIELDS * ROWS, LON),
                coefficients.reshape(6 * ROWS, LON),
                obs_cell.reshape(ROWS, LANE),
                obs_value.reshape(ROWS, LANE),
                obs_weight.reshape(ROWS, LANE),
            )
        ),
        obs_count,
    )
    packed = lax.all_gather(mine, "lat", axis=0, tiled=True)
    spans = [list(range(first, first + SPAN)) for first in range(0, TIMES, SPAN)]
    strides = [list(range(first, TIMES, SPAN)) for first in range(SPAN)]
    sent = pl.pallas_call(
        subwindow_kernel,
        out_shape=jax.ShapeDtypeStruct((SPAN * KINDS * SHARE, LANE), jnp.float32),
        in_specs=[pl.BlockSpec(memory_space=pltpu.SMEM), vmem, vmem],
        out_specs=vmem,
        scratch_shapes=[
            pltpu.VMEM((FIELDS * MID * TILES, SLABS * ROWS * LANE), jnp.bfloat16)
        ],
        compiler_params=limit,
    )(obs_step, packed, correlation[0])
    owned = lax.all_to_all(sent, "tm", 0, 0, axis_index_groups=spans, tiled=True)
    reduced = pl.pallas_call(
        block_kernel,
        out_shape=jax.ShapeDtypeStruct((BLOCKS * MAP_ROWS, LANE), jnp.float32),
        in_specs=[vmem],
        out_specs=vmem,
        compiler_params=limit,
    )(owned)
    quarters = reduced.reshape(BLOCKS, -1, 4, LANE)
    maps = lax.all_to_all(quarters, "tm", 0, 0, axis_index_groups=strides, tiled=True)
    solved = pl.pallas_call(
        time_kernel,
        out_shape=jax.ShapeDtypeStruct((SPAN * 2 * SHARE, LANE), jnp.float32),
        in_specs=[vmem] * 2,
        out_specs=vmem,
        compiler_params=limit,
    )(owned, maps.reshape(BLOCKS * MAP_ROWS, LANE))
    quarters = solved.reshape(SPAN, -1, 4, LANE)
    returned = lax.all_to_all(quarters, "tm", 0, 0, axis_index_groups=spans, tiled=True)
    shape = jax.ShapeDtypeStruct((FIELDS, ROWS, LON), jnp.float32)
    gradient, direction = pl.pallas_call(
        unpack_kernel,
        out_shape=(shape, shape),
        in_specs=[vmem],
        out_specs=(vmem, vmem),
        compiler_params=limit,
    )(returned.reshape(SPAN * 2 * SHARE, LANE))
    return gradient[None], direction[None]


def solution(mesh):
    return jax.shard_map(
        on_device,
        mesh=mesh,
        in_specs=(
            P("tm", None, "lat", None),
            P("tm", None, "lat", None),
            P(None, "lat", None),
            P("tm", "lat"),
            P("tm", "lat"),
            P("tm", "lat"),
            P("tm", "lat"),
            P("tm"),
        ),
        out_specs=(P("tm", None, "lat", None), P("tm", None, "lat", None)),
        check_vma=False,
    )
```

```python
import jax
import jax.numpy as jnp
from jax import lax
from jax.experimental import pallas as pl
from jax.experimental.pallas import tpu as pltpu
from jax.sharding import PartitionSpec as P

STEPS = 4
FIELDS = 4
NY = 32
LON = 384
ROWS = 8
SLABS = 4
WIN = 3 * ROWS
MID = 16
LANE = 128
TILES = LON // LANE
PACK = 11 * ROWS
KINDS = 4
TIMES = 128
SPAN = 16
BLOCKS = TIMES // SPAN
SHARE = FIELDS * ROWS * TILES // SPAN
MAPS = 6
MAP_ROWS = MAPS * SHARE
CHUNK = 512


def lon_roll(field, by):
    return pltpu.roll(field, by % LON, 1)


def row_roll(field, by):
    return pltpu.roll(field, by % field.shape[0], 0)


def step(state, coef, sign):
    h, u, v, q = state
    keep, kx, kw, ky, ks, cx, cw, cy, cs = coef["common"]
    qe, qw, qn, qs = coef["forward" if sign > 0 else "backward"]

    def sides(f):
        return lon_roll(f, -1), lon_roll(f, 1), row_roll(f, -1), row_roll(f, 1)

    def spread(f, e, w, n, s):
        return keep * f + (kx * e + kw * w) + (ky * n + ks * s)

    he, hw, hn, hs = sides(h)
    ue, uw, un, us = sides(u)
    ve, vw, vn, vs = sides(v)
    te, tw, tn, ts = sides(q)
    div = (cw * uw - cx * u) + (cs * vs - cy * v)
    gx = cx * (he - h)
    gy = cy * (hn - h)
    new_h = spread(h, he, hw, hn, hs)
    new_u = spread(u, ue, uw, un, us)
    new_v = spread(v, ve, vw, vn, vs)
    new_q = keep * q + (qe * te + qw * tw) + (qn * tn + qs * ts)
    if sign > 0:
        return new_h + div, new_u - gx, new_v - gy, new_q
    return new_h - div, new_u + gx, new_v + gy, new_q


def split(value):
    big = value.astype(jnp.bfloat16)
    return big, (value - big.astype(jnp.float32)).astype(jnp.bfloat16)


def pack_kernel(inc, coef, cell, value, weight, count, out, cell_buf, weight_buf, sems):
    first = (FIELDS + 6) * ROWS
    moves = (
        (cell, cell_buf),
        (weight, weight_buf),
        (coef, out.at[FIELDS * ROWS : first, :]),
        (inc, out.at[0 : FIELDS * ROWS, :]),
        (value, out.at[first:PACK, LANE : 2 * LANE]),
    )
    copies = [pltpu.make_async_copy(a, b, sems.at[i]) for i, (a, b) in enumerate(moves)]
    for copy in copies:
        copy.start()
    slot = lax.broadcasted_iota(jnp.int32, (ROWS, LANE), 0) * LANE
    slot = slot + lax.broadcasted_iota(jnp.int32, (ROWS, LANE), 1)
    live = slot < count[0, 0]
    for copy in copies[:2]:
        copy.wait()
    out[first:PACK, 0:LANE] = cell_buf[...].astype(jnp.float32)
    out[first:PACK, 2 * LANE :] = jnp.where(live, weight_buf[...], 0.0)
    for copy in copies[2:]:
        copy.wait()


def subwindow_kernel(obs_step, packed, rates, out):
    slab = lax.axis_index("lat")
    obs_at = jnp.broadcast_to(obs_step[...], (WIN, LON))

    def window(base):
        parts = []
        for offset in (-1, 0, 1):
            at = slab + offset
            inside = jnp.logical_and(at >= 0, at < SLABS)
            first = jnp.clip(at, 0, SLABS - 1) * PACK + base
            part = packed[pl.ds(pl.multiple_of(first, ROWS), ROWS), :]
            parts.append(jnp.where(inside, part, 0.0))
        return jnp.concatenate(parts, axis=0)

    row = lax.broadcasted_iota(jnp.int32, (WIN, LON), 0) + (slab - 1) * ROWS
    in_grid = jnp.logical_and(row >= 0, row < NY)
    inc = tuple(window(f * ROWS) for f in range(FIELDS))
    cx, cy, ax, by, kx, ky = (window((FIELDS + i) * ROWS) for i in range(6))

    def south(c):
        return jnp.where(in_grid, row_roll(c, 1), 0.0)

    kw, ks, cw, cs = lon_roll(kx, 1), south(ky), lon_roll(cx, 1), south(cy)
    aw, bs = lon_roll(ax, 1), south(by)
    keep = 1.0 - ((kx + kw) + (ky + ks))
    coef = {
        "common": (keep, kx, kw, ky, ks, cx, cw, cy, cs),
        "forward": (kx - ax, kw + aw, ky - by, ks + bs),
        "backward": (kx + ax, kw - aw, ky + by, ks - bs),
    }
    state = inc
    seen = inc
    for turn in range(STEPS):
        state = step(state, coef, 1.0)
        if turn == 0:
            seen = state
        else:
            seen = tuple(jnp.where(obs_at == turn + 1, a, b) for a, b in zip(state, seen, strict=True))
    end = state

    upper = lax.broadcasted_iota(jnp.int32, (ROWS, LON), 0) < ROWS // 2

    def fold(x):
        ends = jnp.where(upper, x[2 * ROWS :], x[:ROWS])
        return jnp.concatenate([x[ROWS : 2 * ROWS], ends], axis=0)

    inc, end, seen = (tuple(fold(x) for x in fields) for fields in (inc, end, seen))
    coef = {name: tuple(fold(x) for x in coef[name]) for name in ("common", "backward")}
    table = jnp.concatenate(
        [seen[f][:, t * LANE : (t + 1) * LANE] for t in range(TILES) for f in range(FIELDS)], axis=0
    )
    high = table.shape[0]
    table_parts = jnp.concatenate(split(jnp.transpose(table)), axis=0)

    half = jnp.bfloat16
    hi_iota = lax.broadcasted_iota(jnp.int32, (high, CHUNK), 0).astype(half)
    lo_iota = lax.broadcasted_iota(jnp.int32, (LANE, CHUNK), 0)
    lo_half = lo_iota.astype(half)
    one, none = jnp.ones((high, CHUNK), half), jnp.zeros((high, CHUNK), half)
    picks, places = [], []
    for owner in range(SLABS):
        base = owner * PACK + 10 * ROWS
        cell = packed[base : base + ROWS, 0:LANE].astype(jnp.int32)
        value = packed[base : base + ROWS, LANE : 2 * LANE]
        weight = packed[base : base + ROWS, 2 * LANE : 3 * LANE]
        low = jnp.bitwise_and(cell, LANE - 1)
        tile_row = jnp.right_shift(cell, 7)
        field_row = jnp.right_shift(tile_row * 21846, 16)
        tile = tile_row - field_row * TILES
        field = jnp.right_shift(field_row, 5)
        rel = jnp.bitwise_and(field_row, NY - 1) - slab * ROWS
        near = jnp.logical_and(rel >= -(ROWS // 2), rel < ROWS + ROWS // 2)
        place = tile * (FIELDS * MID) + field * MID + jnp.bitwise_and(rel, MID - 1)
        spot = jnp.where(near, place, -1)
        for pair in range(ROWS // 4):
            rows = tuple(range(4 * pair, 4 * pair + 4))
            def wide(x):
                return jnp.concatenate([x[r : r + 1, :] for r in rows], axis=1)

            here, column = wide(spot), wide(low)
            pick = jnp.where(hi_iota == here.astype(half), one, none)
            match = lo_iota == column
            match_half = lo_half == column.astype(half)
            columns = lax.dot_general(
                table_parts, pick, (((1,), (0,)), ((), ())), preferred_element_type=jnp.float32
            )
            columns = columns[:LANE] + columns[LANE:]
            sampled = jnp.sum(jnp.where(match, columns, 0.0), axis=0, keepdims=True)
            depart = wide(weight) * (sampled - wide(value))
            big = depart.astype(half)
            small = (depart - big.astype(jnp.float32)).astype(half)
            placed = jnp.concatenate(
                [jnp.where(match_half, part, none[:LANE]) for part in (big, small)], axis=0
            )
            picks.append(pick)
            places.append(placed)
    forcing = lax.dot_general(
        jnp.concatenate(picks, axis=1),
        jnp.concatenate(places, axis=1),
        (((1,), (1,)), ((), ())),
        preferred_element_type=jnp.float32,
    )
    forcing = forcing[:, :LANE] + forcing[:, LANE:]

    back = inc
    for _ in range(STEPS):
        back = step(back, coef, -1.0)

    inject = tuple(
        jnp.concatenate(
            [
                forcing[(t * FIELDS + f) * MID : (t * FIELDS + f + 1) * MID, :]
                for t in range(TILES)
            ],
            axis=1,
        )
        for f in range(FIELDS)
    )

    def push(state, turn):
        scale = jnp.where(obs_at[:MID] == turn, 1.0, 0.0)
        return tuple(a + scale * b for a, b in zip(state, inject, strict=True))

    follows = jnp.where(lax.axis_index("tm") < TIMES - 1, 1.0, 0.0)
    adjoint = push(tuple(follows * e for e in end), STEPS)
    for turn in range(STEPS):
        adjoint = push(step(adjoint, coef, -1.0), STEPS - 1 - turn)

    mine = slice(0, ROWS)
    for f in range(FIELDS):
        kinds = (inc[f][mine] + adjoint[f][mine], -end[f][mine], -back[f][mine], rates[f])
        half, odd = divmod(f, 2)
        for q, kind in enumerate(kinds):
            for t in range(TILES):
                first = half * ROWS * KINDS * SHARE + q * SHARE + odd * TILES + t
                out[pl.ds(first, ROWS, stride=KINDS * SHARE), :] = kind[:, t * LANE : (t + 1) * LANE]


def load_block(parts):
    def load(i, q):
        first = (i * KINDS + q) * SHARE
        return parts[first : first + SHARE, :]

    x, y, z, c = ([load(i, q) for i in range(SPAN)] for q in range(KINDS))
    g = list(x)
    for i in range(1, SPAN):
        g[i] = g[i] + y[i - 1]
        g[i - 1] = g[i - 1] + z[i]
    return g, y, z, c


def block_kernel(parts, out):
    g, y, z, c = load_block(parts)
    sums, factors = [g[-1]], [jnp.ones_like(g[-1])]
    for i in range(SPAN - 2, -1, -1):
        sums.insert(0, g[i] + c[i + 1] * sums[0])
        factors.insert(0, c[i + 1] * factors[0])
    shares = [1.0 - r * r for r in c]
    own, push = shares[0] * sums[0], shares[0] * factors[0]
    for i in range(1, SPAN):
        own = c[i] * own + shares[i] * sums[i]
        push = c[i] * push + shares[i] * factors[i]
    block = jnp.right_shift(lax.axis_index("tm"), 4)
    terms = (factors[0], c[0], c[0] * sums[0] + z[0], y[-1], push, own)
    for i, term in enumerate(terms):
        out[i * SHARE : (i + 1) * SHARE, :] = term
    whole = out[0:MAP_ROWS, :]
    for b in range(BLOCKS):
        first = b * MAP_ROWS
        if b > 0:
            out[first : first + MAP_ROWS, :] = whole
        first += 4 * SHARE
        out[first : first + SHARE, :] = jnp.where(b < block, z[0], push)


def time_kernel(parts, maps, out):
    block = jnp.right_shift(lax.axis_index("tm"), 4)

    def term(b, i):
        first = b * MAP_ROWS + i * SHARE
        return maps[first : first + SHARE, :]

    factor, first_rate, back, last_y, shared, own = (
        [term(b, i) for b in range(BLOCKS)] for i in range(MAPS)
    )
    through = [r * f for r, f in zip(first_rate, factor, strict=True)]
    edge = [(1.0 - r * r) * f for r, f in zip(first_rate, factor, strict=True)]
    zero = jnp.zeros_like(own[0])
    before = [zero] + last_y[:-1]
    after = shared[1:] + [zero]
    later = [zero]
    for b in range(BLOCKS - 1, 0, -1):
        later.insert(0, (back[b] + first_rate[b] * before[b]) + through[b] * later[0])
    earlier = [zero]
    for b in range(BLOCKS - 1):
        made = (own[b] + shared[b] * later[b]) + edge[b] * before[b]
        earlier.append(made + through[b] * earlier[-1])

    def mine(values):
        picked = values[0]
        for b in range(1, BLOCKS):
            picked = jnp.where(block == b, values[b], picked)
        return picked

    g, _, _, c = load_block(parts)
    g[0] = g[0] + mine(before)
    total = [g[-1] + mine(later)]
    g[-1] = g[-1] + mine(after)
    for i in range(SPAN - 2, -1, -1):
        total.insert(0, g[i] + c[i + 1] * total[0])
    smooth = mine(earlier)
    for i in range(SPAN):
        smooth = c[i] * smooth + (1.0 - c[i] * c[i]) * total[i]
        for e, value in enumerate((g[i], smooth)):
            first = (i * 2 + e) * SHARE
            out[first : first + SHARE, :] = value


def unpack_kernel(parts, gradient, direction):
    for e, out in enumerate((gradient, direction)):
        for f in range(FIELDS):
            half, odd = divmod(f, 2)
            for t in range(TILES):
                first = half * ROWS * 2 * SHARE + e * SHARE + odd * TILES + t
                out[f, :, t * LANE : (t + 1) * LANE] = parts[pl.ds(first, ROWS, stride=2 * SHARE), :]


def on_device(
    increments, correlation, coefficients, obs_cell, obs_value, obs_weight, obs_count, obs_step
):
    vmem = pl.BlockSpec(memory_space=pltpu.VMEM)
    far = pl.BlockSpec(memory_space=pltpu.HBM)
    limit = pltpu.CompilerParams(vmem_limit_bytes=32 * 1024 * 1024)
    mine = pl.pallas_call(
        pack_kernel,
        out_shape=jax.ShapeDtypeStruct((PACK, LON), jnp.float32),
        in_specs=[far] * 5 + [pl.BlockSpec(memory_space=pltpu.SMEM)],
        out_specs=vmem,
        scratch_shapes=[
            pltpu.VMEM((ROWS, LANE), jnp.int32),
            pltpu.VMEM((ROWS, LANE), jnp.float32),
            pltpu.SemaphoreType.DMA((5,)),
        ],
        compiler_params=limit,
    )(
        *(
            pltpu.with_memory_space_constraint(part, pltpu.HBM)
            for part in (
                increments.reshape(FIELDS * ROWS, LON),
                coefficients.reshape(6 * ROWS, LON),
                obs_cell.reshape(ROWS, LANE),
                obs_value.reshape(ROWS, LANE),
                obs_weight.reshape(ROWS, LANE),
            )
        ),
        obs_count,
    )
    packed = lax.all_gather(mine, "lat", axis=0, tiled=True)
    spans = [list(range(first, first + SPAN)) for first in range(0, TIMES, SPAN)]
    strides = [list(range(first, TIMES, SPAN)) for first in range(SPAN)]
    sent = pl.pallas_call(
        subwindow_kernel,
        out_shape=jax.ShapeDtypeStruct((SPAN * KINDS * SHARE, LANE), jnp.float32),
        in_specs=[vmem] * 3,
        out_specs=vmem,
        compiler_params=limit,
    )(obs_step.reshape(1, 1), packed, correlation[0])
    owned = lax.all_to_all(
        sent.reshape(SPAN, -1, 2, LANE), "tm", 0, 0, axis_index_groups=spans, tiled=True
    ).reshape(sent.shape)
    reduced = pl.pallas_call(
        block_kernel,
        out_shape=jax.ShapeDtypeStruct((BLOCKS * MAP_ROWS, LANE), jnp.float32),
        in_specs=[vmem],
        out_specs=vmem,
        compiler_params=limit,
    )(owned)
    quarters = reduced.reshape(BLOCKS, -1, 4, LANE)
    maps = lax.all_to_all(quarters, "tm", 0, 0, axis_index_groups=strides, tiled=True)
    solved = pl.pallas_call(
        time_kernel,
        out_shape=jax.ShapeDtypeStruct((SPAN * 2 * SHARE, LANE), jnp.float32),
        in_specs=[vmem] * 2,
        out_specs=vmem,
        compiler_params=limit,
    )(owned, maps.reshape(BLOCKS * MAP_ROWS, LANE))
    quarters = solved.reshape(SPAN, -1, 4, LANE)
    returned = lax.all_to_all(quarters, "tm", 0, 0, axis_index_groups=spans, tiled=True)
    shape = jax.ShapeDtypeStruct((FIELDS, ROWS, LON), jnp.float32)
    gradient, direction = pl.pallas_call(
        unpack_kernel,
        out_shape=(shape, shape),
        in_specs=[vmem],
        out_specs=(vmem, vmem),
        compiler_params=limit,
    )(returned.reshape(SPAN * 2 * SHARE, LANE))
    return gradient[None], direction[None]


def solution(mesh):
    return jax.shard_map(
        on_device,
        mesh=mesh,
        in_specs=(
            P("tm", None, "lat", None),
            P("tm", None, "lat", None),
            P(None, "lat", None),
            P("tm", "lat"),
            P("tm", "lat"),
            P("tm", "lat"),
            P("tm", "lat"),
            P("tm"),
        ),
        out_specs=(P("tm", None, "lat", None), P("tm", None, "lat", None)),
        check_vma=False,
    )
```

```python
import jax
import jax.numpy as jnp
from jax import lax
from jax.experimental import pallas as pl
from jax.experimental.pallas import tpu as pltpu
from jax.sharding import PartitionSpec as P

STEPS = 4
FIELDS = 4
NY = 32
LON = 384
ROWS = 8
SLABS = 4
WIN = 3 * ROWS
MID = 16
LANE = 128
TILES = LON // LANE
PACK = 11 * ROWS
KINDS = 4
TIMES = 128
SPAN = 16
BLOCKS = TIMES // SPAN
SHARE = FIELDS * ROWS * TILES // SPAN
MAPS = 6
MAP_ROWS = MAPS * SHARE
CHUNK = 512


def lon_roll(field, by):
    return pltpu.roll(field, by % LON, 1)


def row_roll(field, by):
    return pltpu.roll(field, by % field.shape[0], 0)


def step(state, coef, sign):
    h, u, v, q = state
    keep, kx, kw, ky, ks, cx, cw, cy, cs = coef["common"]
    qe, qw, qn, qs = coef["forward" if sign > 0 else "backward"]

    def sides(f):
        return lon_roll(f, -1), lon_roll(f, 1), row_roll(f, -1), row_roll(f, 1)

    def spread(f, e, w, n, s):
        return keep * f + (kx * e + kw * w) + (ky * n + ks * s)

    he, hw, hn, hs = sides(h)
    ue, uw, un, us = sides(u)
    ve, vw, vn, vs = sides(v)
    te, tw, tn, ts = sides(q)
    div = (cw * uw - cx * u) + (cs * vs - cy * v)
    gx = cx * (he - h)
    gy = cy * (hn - h)
    new_h = spread(h, he, hw, hn, hs)
    new_u = spread(u, ue, uw, un, us)
    new_v = spread(v, ve, vw, vn, vs)
    new_q = keep * q + (qe * te + qw * tw) + (qn * tn + qs * ts)
    if sign > 0:
        return new_h + div, new_u - gx, new_v - gy, new_q
    return new_h - div, new_u + gx, new_v + gy, new_q


def split(value):
    big = value.astype(jnp.bfloat16)
    return big, (value - big.astype(jnp.float32)).astype(jnp.bfloat16)


def pack_kernel(inc, coef, cell, value, weight, count, out, cell_buf, weight_buf, sems):
    first = (FIELDS + 6) * ROWS
    moves = (
        (cell, cell_buf),
        (weight, weight_buf),
        (coef, out.at[FIELDS * ROWS : first, :]),
        (inc, out.at[0 : FIELDS * ROWS, :]),
        (value, out.at[first:PACK, LANE : 2 * LANE]),
    )
    copies = [pltpu.make_async_copy(a, b, sems.at[i]) for i, (a, b) in enumerate(moves)]
    for copy in copies:
        copy.start()
    slot = lax.broadcasted_iota(jnp.int32, (ROWS, LANE), 0) * LANE
    slot = slot + lax.broadcasted_iota(jnp.int32, (ROWS, LANE), 1)
    live = slot < count[0, 0]
    for copy in copies[:2]:
        copy.wait()
    out[first:PACK, 0:LANE] = cell_buf[...].astype(jnp.float32)
    out[first:PACK, 2 * LANE :] = jnp.where(live, weight_buf[...], 0.0)
    for copy in copies[2:]:
        copy.wait()


def subwindow_kernel(obs_step, packed, rates, out):
    slab = lax.axis_index("lat")
    obs_at = jnp.broadcast_to(obs_step[...], (WIN, LON))

    def window(base):
        parts = []
        for offset in (-1, 0, 1):
            at = slab + offset
            inside = jnp.logical_and(at >= 0, at < SLABS)
            first = jnp.clip(at, 0, SLABS - 1) * PACK + base
            part = packed[pl.ds(pl.multiple_of(first, ROWS), ROWS), :]
            parts.append(jnp.where(inside, part, 0.0))
        return jnp.concatenate(parts, axis=0)

    row = lax.broadcasted_iota(jnp.int32, (WIN, LON), 0) + (slab - 1) * ROWS
    in_grid = jnp.logical_and(row >= 0, row < NY)
    inc = tuple(window(f * ROWS) for f in range(FIELDS))
    cx, cy, ax, by, kx, ky = (window((FIELDS + i) * ROWS) for i in range(6))

    def south(c):
        return jnp.where(in_grid, row_roll(c, 1), 0.0)

    kw, ks, cw, cs = lon_roll(kx, 1), south(ky), lon_roll(cx, 1), south(cy)
    aw, bs = lon_roll(ax, 1), south(by)
    keep = 1.0 - ((kx + kw) + (ky + ks))
    coef = {
        "common": (keep, kx, kw, ky, ks, cx, cw, cy, cs),
        "forward": (kx - ax, kw + aw, ky - by, ks + bs),
        "backward": (kx + ax, kw - aw, ky + by, ks - bs),
    }
    state = inc
    seen = inc
    for turn in range(STEPS):
        state = step(state, coef, 1.0)
        if turn == 0:
            seen = state
        else:
            seen = tuple(jnp.where(obs_at == turn + 1, a, b) for a, b in zip(state, seen, strict=True))
    end = state

    upper = lax.broadcasted_iota(jnp.int32, (ROWS, LON), 0) < ROWS // 2

    def fold(x):
        ends = jnp.where(upper, x[2 * ROWS :], x[:ROWS])
        return jnp.concatenate([x[ROWS : 2 * ROWS], ends], axis=0)

    inc, end, seen = (tuple(fold(x) for x in fields) for fields in (inc, end, seen))
    coef = {name: tuple(fold(x) for x in coef[name]) for name in ("common", "backward")}
    table = jnp.concatenate(
        [seen[f][:, t * LANE : (t + 1) * LANE] for t in range(TILES) for f in range(FIELDS)], axis=0
    )
    high = table.shape[0]
    table_parts = jnp.concatenate(split(jnp.transpose(table)), axis=0)

    half = jnp.bfloat16
    hi_iota = lax.broadcasted_iota(jnp.int32, (high, CHUNK), 0).astype(half)
    lo_iota = lax.broadcasted_iota(jnp.int32, (LANE, CHUNK), 0)
    lo_half = lo_iota.astype(half)
    one, none = jnp.ones((high, CHUNK), half), jnp.zeros((high, CHUNK), half)
    picks, places = [], []
    for owner in range(SLABS):
        base = owner * PACK + 10 * ROWS
        cell = packed[base : base + ROWS, 0:LANE].astype(jnp.int32)
        value = packed[base : base + ROWS, LANE : 2 * LANE]
        weight = packed[base : base + ROWS, 2 * LANE : 3 * LANE]
        low = jnp.bitwise_and(cell, LANE - 1)
        tile_row = jnp.right_shift(cell, 7)
        field_row = jnp.right_shift(tile_row * 21846, 16)
        tile = tile_row - field_row * TILES
        field = jnp.right_shift(field_row, 5)
        rel = jnp.bitwise_and(field_row, NY - 1) - slab * ROWS
        near = jnp.logical_and(rel >= -(ROWS // 2), rel < ROWS + ROWS // 2)
        place = tile * (FIELDS * MID) + field * MID + jnp.bitwise_and(rel, MID - 1)
        spot = jnp.where(near, place, -1)
        for pair in range(ROWS // 4):
            rows = tuple(range(4 * pair, 4 * pair + 4))
            def wide(x):
                return jnp.concatenate([x[r : r + 1, :] for r in rows], axis=1)

            here, column = wide(spot), wide(low)
            pick = jnp.where(hi_iota == here.astype(half), one, none)
            match = lo_iota == column
            match_half = lo_half == column.astype(half)
            columns = lax.dot_general(
                table_parts, pick, (((1,), (0,)), ((), ())), preferred_element_type=jnp.float32
            )
            columns = columns[:LANE] + columns[LANE:]
            sampled = jnp.sum(jnp.where(match, columns, 0.0), axis=0, keepdims=True)
            depart = wide(weight) * (sampled - wide(value))
            big = depart.astype(half)
            small = (depart - big.astype(jnp.float32)).astype(half)
            placed = jnp.concatenate(
                [jnp.where(match_half, part, none[:LANE]) for part in (big, small)], axis=0
            )
            picks.append(pick)
            places.append(placed)
    forcing = lax.dot_general(
        jnp.concatenate(picks, axis=1),
        jnp.concatenate(places, axis=1),
        (((1,), (1,)), ((), ())),
        preferred_element_type=jnp.float32,
    )
    forcing = forcing[:, :LANE] + forcing[:, LANE:]

    back = inc
    for _ in range(STEPS):
        back = step(back, coef, -1.0)

    inject = tuple(
        jnp.concatenate(
            [
                forcing[(t * FIELDS + f) * MID : (t * FIELDS + f + 1) * MID, :]
                for t in range(TILES)
            ],
            axis=1,
        )
        for f in range(FIELDS)
    )

    def push(state, turn):
        scale = jnp.where(obs_at[:MID] == turn, 1.0, 0.0)
        return tuple(a + scale * b for a, b in zip(state, inject, strict=True))

    follows = jnp.where(lax.axis_index("tm") < TIMES - 1, 1.0, 0.0)
    adjoint = push(tuple(follows * e for e in end), STEPS)
    for turn in range(STEPS):
        adjoint = push(step(adjoint, coef, -1.0), STEPS - 1 - turn)

    mine = slice(0, ROWS)
    for f in range(FIELDS):
        kinds = (inc[f][mine] + adjoint[f][mine], -end[f][mine], -back[f][mine], rates[f])
        half, odd = divmod(f, 2)
        for q, kind in enumerate(kinds):
            for t in range(TILES):
                first = half * ROWS * KINDS * SHARE + q * SHARE + odd * TILES + t
                out[pl.ds(first, ROWS, stride=KINDS * SHARE), :] = kind[:, t * LANE : (t + 1) * LANE]


def load_block(parts):
    def load(i, q):
        first = (i * KINDS + q) * SHARE
        return parts[first : first + SHARE, :]

    x, y, z, c = ([load(i, q) for i in range(SPAN)] for q in range(KINDS))
    g = list(x)
    for i in range(1, SPAN):
        g[i] = g[i] + y[i - 1]
        g[i - 1] = g[i - 1] + z[i]
    return g, y, z, c


def block_kernel(parts, out):
    g, y, z, c = load_block(parts)
    sums, factors = [g[-1]], [jnp.ones_like(g[-1])]
    for i in range(SPAN - 2, -1, -1):
        sums.insert(0, g[i] + c[i + 1] * sums[0])
        factors.insert(0, c[i + 1] * factors[0])
    shares = [1.0 - r * r for r in c]
    own, push = shares[0] * sums[0], shares[0] * factors[0]
    for i in range(1, SPAN):
        own = c[i] * own + shares[i] * sums[i]
        push = c[i] * push + shares[i] * factors[i]
    block = jnp.right_shift(lax.axis_index("tm"), 4)
    terms = (factors[0], c[0], c[0] * sums[0] + z[0], y[-1], push, own)
    for i, term in enumerate(terms):
        out[i * SHARE : (i + 1) * SHARE, :] = term
    whole = out[0:MAP_ROWS, :]
    for b in range(BLOCKS):
        first = b * MAP_ROWS
        if b > 0:
            out[first : first + MAP_ROWS, :] = whole
        first += 4 * SHARE
        out[first : first + SHARE, :] = jnp.where(b < block, z[0], push)


def time_kernel(parts, maps, out):
    block = jnp.right_shift(lax.axis_index("tm"), 4)

    def term(b, i):
        first = b * MAP_ROWS + i * SHARE
        return maps[first : first + SHARE, :]

    factor, first_rate, back, last_y, shared, own = (
        [term(b, i) for b in range(BLOCKS)] for i in range(MAPS)
    )
    through = [r * f for r, f in zip(first_rate, factor, strict=True)]
    edge = [(1.0 - r * r) * f for r, f in zip(first_rate, factor, strict=True)]
    zero = jnp.zeros_like(own[0])
    before = [zero] + last_y[:-1]
    after = shared[1:] + [zero]
    later = [zero]
    for b in range(BLOCKS - 1, 0, -1):
        later.insert(0, (back[b] + first_rate[b] * before[b]) + through[b] * later[0])
    earlier = [zero]
    for b in range(BLOCKS - 1):
        made = (own[b] + shared[b] * later[b]) + edge[b] * before[b]
        earlier.append(made + through[b] * earlier[-1])

    def mine(values):
        picked = values[0]
        for b in range(1, BLOCKS):
            picked = jnp.where(block == b, values[b], picked)
        return picked

    g, _, _, c = load_block(parts)
    g[0] = g[0] + mine(before)
    total = [g[-1] + mine(later)]
    g[-1] = g[-1] + mine(after)
    for i in range(SPAN - 2, -1, -1):
        total.insert(0, g[i] + c[i + 1] * total[0])
    smooth = mine(earlier)
    for i in range(SPAN):
        smooth = c[i] * smooth + (1.0 - c[i] * c[i]) * total[i]
        for e, value in enumerate((g[i], smooth)):
            first = (i * 2 + e) * SHARE
            out[first : first + SHARE, :] = value


def unpack_kernel(parts, gradient, direction, held, sems):
    copies = []
    for e, out in enumerate((gradient, direction)):
        for f in range(FIELDS):
            half, odd = divmod(f, 2)
            for t in range(TILES):
                first = half * ROWS * 2 * SHARE + e * SHARE + odd * TILES + t
                tile = parts[pl.ds(first, ROWS, stride=2 * SHARE), :]
                held[e, f, :, t * LANE : (t + 1) * LANE] = tile
        copies.append(pltpu.make_async_copy(held.at[e], out, sems.at[e]))
        copies[-1].start()
    for copy in copies:
        copy.wait()


def on_device(
    increments, correlation, coefficients, obs_cell, obs_value, obs_weight, obs_count, obs_step
):
    vmem = pl.BlockSpec(memory_space=pltpu.VMEM)
    far = pl.BlockSpec(memory_space=pltpu.HBM)
    limit = pltpu.CompilerParams(vmem_limit_bytes=32 * 1024 * 1024)
    mine = pl.pallas_call(
        pack_kernel,
        out_shape=jax.ShapeDtypeStruct((PACK, LON), jnp.float32),
        in_specs=[far] * 5 + [pl.BlockSpec(memory_space=pltpu.SMEM)],
        out_specs=vmem,
        scratch_shapes=[
            pltpu.VMEM((ROWS, LANE), jnp.int32),
            pltpu.VMEM((ROWS, LANE), jnp.float32),
            pltpu.SemaphoreType.DMA((5,)),
        ],
        compiler_params=limit,
    )(
        *(
            pltpu.with_memory_space_constraint(part, pltpu.HBM)
            for part in (
                increments.reshape(FIELDS * ROWS, LON),
                coefficients.reshape(6 * ROWS, LON),
                obs_cell.reshape(ROWS, LANE),
                obs_value.reshape(ROWS, LANE),
                obs_weight.reshape(ROWS, LANE),
            )
        ),
        obs_count,
    )
    packed = lax.all_gather(mine, "lat", axis=0, tiled=True)
    spans = [list(range(first, first + SPAN)) for first in range(0, TIMES, SPAN)]
    strides = [list(range(first, TIMES, SPAN)) for first in range(SPAN)]
    sent = pl.pallas_call(
        subwindow_kernel,
        out_shape=jax.ShapeDtypeStruct((SPAN * KINDS * SHARE, LANE), jnp.float32),
        in_specs=[vmem] * 3,
        out_specs=vmem,
        compiler_params=limit,
    )(obs_step.reshape(1, 1), packed, correlation[0])
    owned = lax.all_to_all(sent, "tm", 0, 0, axis_index_groups=spans, tiled=True)
    reduced = pl.pallas_call(
        block_kernel,
        out_shape=jax.ShapeDtypeStruct((BLOCKS * MAP_ROWS, LANE), jnp.float32),
        in_specs=[vmem],
        out_specs=vmem,
        compiler_params=limit,
    )(owned)
    quarters = reduced.reshape(BLOCKS, -1, 4, LANE)
    maps = lax.all_to_all(quarters, "tm", 0, 0, axis_index_groups=strides, tiled=True)
    solved = pl.pallas_call(
        time_kernel,
        out_shape=jax.ShapeDtypeStruct((SPAN * 2 * SHARE, LANE), jnp.float32),
        in_specs=[vmem] * 2,
        out_specs=vmem,
        compiler_params=limit,
    )(owned, maps.reshape(BLOCKS * MAP_ROWS, LANE))
    quarters = solved.reshape(SPAN, -1, 4, LANE)
    returned = lax.all_to_all(quarters, "tm", 0, 0, axis_index_groups=spans, tiled=True)
    shape = jax.ShapeDtypeStruct((FIELDS, ROWS, LON), jnp.float32)
    gradient, direction = pl.pallas_call(
        unpack_kernel,
        out_shape=(shape, shape),
        in_specs=[vmem],
        out_specs=(far, far),
        scratch_shapes=[
            pltpu.VMEM((2, FIELDS, ROWS, LON), jnp.float32),
            pltpu.SemaphoreType.DMA((2,)),
        ],
        compiler_params=limit,
    )(returned.reshape(SPAN * 2 * SHARE, LANE))
    return gradient[None], direction[None]


def solution(mesh):
    return jax.shard_map(
        on_device,
        mesh=mesh,
        in_specs=(
            P("tm", None, "lat", None),
            P("tm", None, "lat", None),
            P(None, "lat", None),
            P("tm", "lat"),
            P("tm", "lat"),
            P("tm", "lat"),
            P("tm", "lat"),
            P("tm"),
        ),
        out_specs=(P("tm", None, "lat", None), P("tm", None, "lat", None)),
        check_vma=False,
    )
```
